512 devices in a mesh: row: 128 (over z, y, core), head: 4 (over x).
Axes of the slice: x: 4, y: 4, z: 16, core: 2. Of those that a mesh axis runs over, the one named last changes fastest.
Arguments:
- residual: bfloat16 [3072, 2048], P('row'), may hold values from -3 to 3
- queries: bfloat16 [3072, 1024], P('row', 'head'), may hold values from -6 to 6
- keys: bfloat16 [3072, 1024], P('row', 'head'), may hold values from -6 to 6
- values: bfloat16 [3072, 2048], P('row', 'head'), may hold values from -6 to 6
- out_gate: bfloat16 [3072, 2048], P('row', 'head'), may hold values from -6 to 6
- decay_input: float32 [3072, 16], P('row', 'head'), may hold values from -4 to 4
- beta_input: float32 [3072, 16], P('row', 'head'), may hold values from -6 to 6
- decay_log: float32 [16], P('head'), may hold values from -1.5 to 1.5
- decay_bias: float32 [16], P('head'), may hold values from -1 to 1
- past_state: bfloat16 [3072, 16, 128, 128], P('row', 'head'), may hold values from -2 to 2
- head_norm: float32 [128], replicated, may hold values from 0.1 to 1.9
- out_proj: bfloat16 [2048, 2048], P('head'), may hold values from -0.125 to 0.125
- post_norm: float32 [2048], replicated, may hold values from 0.1 to 1.9
- expert_ids: int32 [3072, 10], P('row'), may hold values from 0 to 255, as said below
- expert_gates: float32 [3072, 10], P('row'), may hold values from 0.1 to 1
- capacity: int32 [256], replicated, may hold values from 60 to 239
- gate_proj: bfloat16 [128, 2048, 512], P('row', None, 'head'), may hold values from -0.125 to 0.125
- up_proj: bfloat16 [128, 2048, 512], P('row', None, 'head'), may hold values from -0.125 to 0.125
- down_proj: bfloat16 [128, 512, 2048], P('row', 'head'), may hold values from -0.375 to 0.375
Outputs:
- mixed: bfloat16 [3072, 2048], P(('row', 'head'))
The draws below stay inside these ranges and needn't reach their ends.
Inputs may be any that keep to these rules, and one draw needn't show every extreme that they name: `expert_ids`: each row names 10 different experts. Among the rows of one index of row no expert is named by more than 2 rows, and some expert by exactly 2. Counts of choices may travel packed several to a 32-bit word.
All inputs are finite; a program needn't handle non-finite values.
Results may differ from the reference program's by a relative error of at most 0.0085.
Values may be sent and summed in bfloat16 or wider, within the bound.
A program may use at most 64 MiB of HBM per device.

```python
import math
import jax
import jax.numpy as jnp
from jax import lax

D = 2048
DK = 128
DV = 128
VH = 16
QKH = 8
HID = 256
TOPK = 10
ROW_DEV = 24
ROWS = 3072
EXPERTS = 256
MOST = 2
MEAN_LOAD = 120


def expert_order(key):
    return jax.random.permutation(key, EXPERTS).astype(jnp.int32)


def draw_expert_ids(key, part):
    order = expert_order(key)
    key = jax.random.fold_in(key, 11)
    hot_count = max(1, EXPERTS // 16)
    blocks = ROWS // ROW_DEV
    period = (ROW_DEV * TOPK + MOST - 1) // MOST
    is_hot = jnp.zeros((EXPERTS,), jnp.int32).at[order[:hot_count]].set(1)
    key_base, key_boost = jax.random.split(key)
    base = jax.random.randint(key_base, (blocks, EXPERTS), 0, 65536, dtype=jnp.int32)
    boost = (jax.random.randint(key_boost, (blocks, EXPERTS), 0, 10, dtype=jnp.int32) < 9).astype(jnp.int32) * is_hot[None, :]
    score = (base + boost * 65536) * EXPERTS + jnp.arange(EXPERTS, dtype=jnp.int32)[None, :]
    ranked = jnp.argsort(-score, axis=1).astype(jnp.int32)
    places = jnp.arange(ROW_DEV * TOPK, dtype=jnp.int32) % period
    chosen = jnp.take(ranked, places, axis=1)
    return chosen.reshape(ROWS, TOPK).astype(jnp.int32)


def draw_capacity(key, part):
    order = expert_order(key)
    key = jax.random.fold_in(key, 12)
    hot_count = max(1, EXPERTS // 16)
    key_cold, key_warm = jax.random.split(key)
    cold = jax.random.randint(key_cold, (EXPERTS,), MEAN_LOAD // 2, 2 * MEAN_LOAD, dtype=jnp.int32)
    warm = jax.random.randint(key_warm, (EXPERTS,), MEAN_LOAD * 9 // 8, MEAN_LOAD * 5 // 4 + 1, dtype=jnp.int32)
    position = jnp.zeros((EXPERTS,), jnp.int32).at[order].set(jnp.arange(EXPERTS, dtype=jnp.int32))
    limit = jnp.where(position < hot_count, warm, cold)
    limit = jnp.where(position == hot_count, 2 * MEAN_LOAD - 1, limit)
    limit = jnp.where(position == hot_count + 1, MEAN_LOAD // 2, limit)
    return limit.astype(jnp.int32)


def block_scale(stream_key, dims, cuts, low, high):
    factor_of, own = 1.0, jax.random.fold_in(stream_key, 6)
    for axis_at, shards_of in cuts:
        steps = jnp.exp(jax.random.uniform(jax.random.fold_in(own, axis_at), (shards_of,), jnp.float32, low / len(cuts), high / len(cuts)))
        factor_of = factor_of * jnp.repeat(steps, dims[axis_at] // shards_of).reshape([-1 if axis == axis_at else 1 for axis in range(len(dims))])
    return factor_of


def gaussian(own_key, extent, spread, most, cuts=(), kind=jnp.bfloat16):
    drawn = jax.random.normal(own_key, extent, jnp.float32) * spread
    if len(cuts) > 0:
        drawn = block_scale(own_key, extent, cuts, -0.22, 0.18) * drawn
    return jnp.clip(drawn, min=-most, max=most).astype(kind)


def setup_inputs(seed: int = 0) -> dict:
    streams_of = jax.random.split(jax.random.key(seed), 20)
    return {
        "residual": gaussian(streams_of[0], (ROWS, D), 0.5, 3.0, ((0, 128),)),
        "queries": gaussian(streams_of[1], (ROWS, QKH * DK), 1.0, 6.0, ((0, 128), (1, 4))),
        "keys": gaussian(streams_of[2], (ROWS, QKH * DK), 1.0, 6.0, ((0, 128), (1, 4))),
        "values": gaussian(streams_of[3], (ROWS, VH * DV), 1.0, 6.0, ((0, 128), (1, 4))),
        "out_gate": gaussian(streams_of[4], (ROWS, VH * DV), 1.0, 6.0, ((0, 128), (1, 4))),
        "decay_input": gaussian(streams_of[5], (ROWS, VH), 1.0, 4.0, ((0, 128), (1, 4)), jnp.float32),
        "beta_input": gaussian(streams_of[6], (ROWS, VH), 1.5, 6.0, ((0, 128), (1, 4)), jnp.float32),
        "decay_log": jnp.clip(jax.random.uniform(streams_of[7], (VH,), jnp.float32, -1.5, 1.5) * block_scale(streams_of[7], (VH,), ((0, 4),), -0.4, 0.0), -1.5, 1.5),
        "decay_bias": jnp.clip(jax.random.uniform(streams_of[8], (VH,), jnp.float32, -1.0, 1.0) * block_scale(streams_of[8], (VH,), ((0, 4),), -0.4, 0.0), -1.0, 1.0),
        "past_state": gaussian(streams_of[9], (ROWS, VH, DK, DV), 0.3, 2.0, ((0, 128), (1, 4))),
        "head_norm": jnp.clip(1.0 + 0.18 * jax.random.normal(streams_of[10], (DV,), jnp.float32), 0.1, 1.9),
        "out_proj": gaussian(streams_of[11], (VH * DV, D), (VH * DV) ** -0.5, 0.125, ((0, 4),)),
        "post_norm": jnp.clip(1.0 + 0.18 * jax.random.normal(streams_of[12], (D,), jnp.float32), 0.1, 1.9),
        "expert_ids": draw_expert_ids(jax.random.fold_in(streams_of[19], 71), 0),
        "expert_gates": jnp.clip(jnp.exp(math.log(1.0) - 2.3025851 * jax.random.uniform(streams_of[14], (ROWS, TOPK), jnp.float32) ** block_scale(streams_of[14], (ROWS, TOPK), ((0, 128),), -0.2, 0.2)), 0.1, 1.0),
        "capacity": draw_capacity(jax.random.fold_in(streams_of[19], 71), 0),
        "gate_proj": gaussian(streams_of[16], (EXPERTS // 2, D, 2 * HID), D ** -0.5, 0.125, ((0, 128), (2, 4))),
        "up_proj": gaussian(streams_of[17], (EXPERTS // 2, D, 2 * HID), D ** -0.5, 0.125, ((0, 128), (2, 4))),
        "down_proj": gaussian(streams_of[18], (EXPERTS // 2, 2 * HID, D), HID ** -0.5, 0.375, ((0, 128), (1, 4))),
    }


def unit_rows(block):
    return block * lax.rsqrt(lax.optimization_barrier(jnp.sum(block * block, axis=-1, keepdims=True)) + 1e-06)

def scaled_rms(block, weight):
    return block * lax.rsqrt(lax.optimization_barrier(jnp.mean(block * block, axis=-1, keepdims=True)) + 1e-06) * weight

def reference(residual, queries, keys, values, out_gate, decay_input, beta_input, decay_log, decay_bias, past_state, head_norm, out_proj, post_norm, expert_ids, expert_gates, capacity, gate_proj, up_proj, down_proj):
    ratio = VH // QKH
    q_unit = unit_rows(queries.astype(jnp.float32).reshape(ROWS, QKH, DK)) * DK ** (-0.5)
    k_unit = unit_rows(keys.astype(jnp.float32).reshape(ROWS, QKH, DK))
    value_all = values.astype(jnp.float32).reshape(ROWS, VH, DV)
    gate_all = out_gate.astype(jnp.float32).reshape(ROWS, VH, DV)
    decay = jnp.exp(-jnp.exp(decay_log)[None, :] * jax.nn.softplus(decay_input + decay_bias[None, :]))
    beta = jax.nn.sigmoid(beta_input)

    def one_head(head):
        state = lax.dynamic_index_in_dim(past_state, head, 1, keepdims=False).astype(jnp.float32)
        group = (head // ratio).astype(jnp.int32)
        query = lax.dynamic_index_in_dim(q_unit, group, 1, keepdims=False)
        key = lax.dynamic_index_in_dim(k_unit, group, 1, keepdims=False)
        read_q = jnp.einsum('rij,ri->rj', state, query, precision=lax.Precision.HIGHEST)
        read_k = jnp.einsum('rij,ri->rj', state, key, precision=lax.Precision.HIGHEST)
        rate = lax.dynamic_index_in_dim(decay, head, 1, keepdims=True)
        strength = lax.dynamic_index_in_dim(beta, head, 1, keepdims=True)
        value = lax.dynamic_index_in_dim(value_all, head, 1, keepdims=False)
        gate = lax.dynamic_index_in_dim(gate_all, head, 1, keepdims=False)
        update = strength * (value - rate * read_k)
        head_out = rate * read_q + lax.optimization_barrier(jnp.sum(key * query, axis=-1, keepdims=True)) * update
        return (scaled_rms(head_out, head_norm) * jax.nn.silu(gate)).astype(jnp.bfloat16)
    gated = lax.map(one_head, jnp.arange(VH, dtype=jnp.int32))
    gated = jnp.transpose(gated, (1, 0, 2)).reshape(ROWS, VH * DV)
    stream = residual.astype(jnp.float32) + jnp.dot(gated, out_proj, preferred_element_type=jnp.float32)
    normed = scaled_rms(stream, post_norm).astype(jnp.bfloat16)
    flat_ids = expert_ids.reshape(-1)
    picks = (flat_ids[:, None] == jnp.arange(EXPERTS, dtype=jnp.int32)[None, :]).astype(jnp.int32)
    rank = lax.optimization_barrier(jnp.sum((jnp.cumsum(picks, axis=0) - picks) * picks, axis=1))
    limit = capacity[flat_ids]
    cap_most = 2 * MEAN_LOAD
    slot = jnp.where(rank < limit, rank, cap_most).astype(jnp.int32)
    row_index = (jnp.arange(ROWS * TOPK, dtype=jnp.int32) // TOPK).astype(jnp.int32)
    table_rows = jnp.zeros((EXPERTS, cap_most), jnp.int32).at[flat_ids, slot].set(row_index, mode='drop')
    table_gate = jnp.zeros((EXPERTS, cap_most), jnp.float32).at[flat_ids, slot].set(expert_gates.reshape(-1), mode='drop')
    half = HID // 2

    def one_expert(expert):
        picked = normed[table_rows[expert]]
        gate_pair = lax.dynamic_index_in_dim(gate_proj, expert // 2, 0, keepdims=False)
        up_pair = lax.dynamic_index_in_dim(up_proj, expert // 2, 0, keepdims=False)
        down_pair = lax.dynamic_index_in_dim(down_proj, expert // 2, 0, keepdims=False)
        total = jnp.zeros((cap_most, D), jnp.float32)
        for part in range(2):
            start = (expert % 2 * HID + part * half).astype(jnp.int32)
            gate_val = jnp.dot(picked, lax.dynamic_slice_in_dim(gate_pair, start, half, 1), preferred_element_type=jnp.float32)
            up_val = jnp.dot(picked, lax.dynamic_slice_in_dim(up_pair, start, half, 1), preferred_element_type=jnp.float32)
            inner = (jax.nn.silu(gate_val) * up_val).astype(jnp.bfloat16)
            part_out = jnp.dot(inner, lax.dynamic_slice_in_dim(down_pair, start, half, 0), preferred_element_type=jnp.float32).astype(jnp.bfloat16)
            total = total + lax.optimization_barrier(part_out).astype(jnp.float32)
        return total * table_gate[expert][:, None]
    outputs = lax.map(one_expert, jnp.arange(EXPERTS, dtype=jnp.int32))
    moe = jnp.zeros((ROWS, D), jnp.float32).at[table_rows.reshape(-1)].add(outputs.reshape(-1, D))
    return (stream + moe).astype(jnp.bfloat16)
```

```python
import jax
import jax.numpy as jnp
from jax import lax
from jax.experimental import pallas as pl
from jax.experimental.pallas import tpu as pltpu
from jax.sharding import PartitionSpec as P

MESH = pl.DeviceIdType.MESH
BF = jnp.bfloat16
F32 = jnp.float32
HIGH = lax.Precision.HIGHEST

ROWS = 24
TOPK = 10
HEADS = 4
DX = 512
CH, CW = 48, 256
STEP = 4

ORDER = (0, -1, 1, -2, 2, -3, 3, -4, 4, -5, 5, -6, 6, -7, 7, -8)
PLACE = {delta: place for place, delta in enumerate(ORDER)}
DIRECT = (-6, 5, -3, 3, -1, 1)
RELAY = {-2: -1, 2: 1, -4: -3, -5: -3, 4: 3, 6: 5, 7: 5, -7: -6, -8: -6}
REACH = (-6, -5, -3, -2, -1, 1, 2, 3, 5, 6)
N_SEM = 128


def dot(a, b):
    return jnp.dot(a, b, preferred_element_type=F32)


def iota(shape, dim):
    return lax.broadcasted_iota(jnp.int32, shape, dim)


def sigmoid(v):
    return 1.0 / (1.0 + jnp.exp(-v))


def kernel(
    res_ref, q_ref, k_ref, v_ref, og_ref, di_ref, bi_ref, dl_ref, db_ref, hn_ref, pn_ref,
    ids_ref, eg_ref, cap_ref, state_hbm, op_hbm, gp_hbm, up_hbm, dp_hbm,
    out_ref,
    ST, OP, W, D, MG, AQ, RD, AP, AR, SM, G, PTL, PTR, PL, PR, S, R, GM, GS, KW,
    MS, MR, SSB, SSR, IN, Y, R2, C, CB, T, FX, FO,
    ss, rs, ls,
):
    row = lax.axis_index("row")
    x = lax.axis_index("head")
    z = row // 8
    me = row % 8
    xs = [x] + [(x + k) % 4 for k in range(1, 4)]
    ds = [me] + [(me + k) % 8 for k in range(1, 8)]

    def at_z(off):
        return (((z + 16 + off) % 16) * 8 + me, x)

    def at_y(k):
        return (z * 8 + ds[k], x)

    def at_x(k):
        return (row, xs[k])

    sent = []

    def remote(src, dst, device):
        n = len(sent)
        copy = pltpu.make_async_remote_copy(
            src_ref=src, dst_ref=dst, send_sem=ss.at[n], recv_sem=rs.at[n], device_id=device, device_id_type=MESH
        )
        copy.start()
        sent.append(copy)
        return copy

    n_local = [0]

    def local(src, dst):
        copy = pltpu.make_async_copy(src, dst, ls.at[n_local[0]])
        n_local[0] += 1
        copy.start()
        return copy

    def x_cols(k):
        return pl.ds(pl.multiple_of(xs[k] * DX, DX), DX)

    states = [local(state_hbm.at[pl.ds(STEP * i, STEP)], ST.at[pl.ds(STEP * i, STEP)]) for i in range(ROWS // STEP)]
    projs = [local(op_hbm.at[:, x_cols(k)], OP.at[k]) for k in (2, 1, 3, 0)]
    own_w = [
        local(gp_hbm.at[0, x_cols(0), :], W.at[x, :, pl.ds(0, 128)]),
        local(up_hbm.at[0, x_cols(0), :], W.at[x, :, pl.ds(128, 128)]),
        local(dp_hbm.at[0, :, x_cols(0)], D.at[x]),
    ]

    barrier = pltpu.get_barrier_semaphore()
    peers = [at_z(off) for off in REACH] + [at_y(k) for k in range(1, 8)] + [at_x(k) for k in range(1, 4)]
    for device in peers:
        pl.semaphore_signal(barrier, inc=1, device_id=device, device_id_type=MESH)
    pl.semaphore_wait(barrier, len(peers))

    def direct(buf):
        return {a: remote(buf.at[0], buf.at[PLACE[a]], at_z(-a)) for a in DIRECT}

    def relay(buf, copies, via):
        copies[via].wait_recv()
        for delta, v in RELAY.items():
            if v == via:
                copies[delta] = remote(buf.at[PLACE[v]], buf.at[PLACE[delta]], at_z(v - delta))

    MG[0] = jnp.concatenate([ids_ref[...].astype(F32), eg_ref[...], jnp.zeros((ROWS, 128 - 2 * TOPK), F32)], axis=1)
    meta = direct(MG)

    moved_w = []
    for k in (2, 1, 3):
        moved_w.append(remote(gp_hbm.at[0, x_cols(k), :], W.at[x, :, pl.ds(0, 128)], at_x(k)))
        moved_w.append(remote(up_hbm.at[0, x_cols(k), :], W.at[x, :, pl.ds(128, 128)], at_x(k)))

    q_unit, k_unit, cross = [], [], []
    for g in range(2):
        for ref, scale, units, base in ((q_ref, 128 ** (-0.5), q_unit, 0), (k_ref, 1.0, k_unit, 2)):
            block = ref[:, 128 * g : 128 * g + 128].astype(F32)
            unit = block * (lax.rsqrt(jnp.sum(block * block, axis=1, keepdims=True) + 1e-06) * scale)
            high = unit.astype(BF).astype(F32)
            AQ[g, pl.ds(base, ROWS, stride=8), :] = high
            AQ[g, pl.ds(base + 1, ROWS, stride=8), :] = unit - high
            units.append(unit)
        for spare in range(4, 8):
            AQ[g, pl.ds(spare, ROWS, stride=8), :] = jnp.zeros((ROWS, 128), F32)
        cross.append(jnp.sum(q_unit[g] * k_unit[g], axis=1, keepdims=True))

    def read_rows(i):
        for u in range(STEP):
            r = STEP * i + u
            at = pl.ds(pl.multiple_of(r * 8, 8), 8)
            for g in range(2):
                a = AQ[g, at, :].astype(BF)
                for h in (2 * g, 2 * g + 1):
                    RD[h, at, :] = dot(a, ST[r, h])

    for i in range(3):
        states[i].wait()
    pl.loop(0, 3)(read_rows)
    for via in (-1, 1, -3, 3, 5, -6):
        relay(MG, meta, via)
    for i in range(3, 6):
        states[i].wait()
    pl.loop(3, 6)(read_rows)

    gated = []
    for h in range(HEADS):
        g = h // 2
        read_q = RD[h, pl.ds(0, ROWS, stride=8), :] + RD[h, pl.ds(1, ROWS, stride=8), :]
        read_k = RD[h, pl.ds(2, ROWS, stride=8), :] + RD[h, pl.ds(3, ROWS, stride=8), :]
        arg = di_ref[:, h : h + 1] + db_ref[:, h : h + 1]
        soft = jnp.maximum(arg, 0.0) + jnp.log(1.0 + jnp.exp(-jnp.abs(arg)))
        decay = jnp.exp(-jnp.exp(dl_ref[:, h : h + 1]) * soft)
        beta = sigmoid(bi_ref[:, h : h + 1])
        cols = slice(128 * h, 128 * h + 128)
        update = beta * (v_ref[:, cols].astype(F32) - decay * read_k)
        head_out = decay * read_q + cross[g] * update
        norm = head_out * lax.rsqrt(jnp.mean(head_out * head_out, axis=1, keepdims=True) + 1e-06) * hn_ref[...]
        gate = og_ref[:, cols].astype(F32)
        gated.append((norm * (gate * sigmoid(gate))).astype(BF))
    gated = jnp.concatenate(gated, axis=1)

    moved_a = {}
    for copy, k in zip(projs, (2, 1, 3, 0)):
        copy.wait()
        AP[k] = dot(gated, OP[k])
        if k:
            moved_a[k] = remote(AP.at[k], AR.at[k - 1], at_x(k))
    for k in (2, 1, 3):
        moved_w.append(remote(dp_hbm.at[0, :, x_cols(k)], D.at[x], at_x(k)))

    for delta in RELAY:
        meta[delta].wait_recv()
    lower = (iota((ROWS, ROWS), 0) > iota((ROWS, ROWS), 1)).astype(F32).astype(BF)
    lane = iota((ROWS, 256), 1)
    lane_expert = (16 * z + 2 * (lane // 32) + (lane // 16) % 2).astype(F32)
    lane_place = (lane // 2) % 8
    lane_slot = (lane % 2).astype(F32)
    for h in range(2):

        def slots_of(j, total, h=h):
            info = MG[8 * h + j]
            match = jnp.zeros((ROWS, 256), F32)
            gates = jnp.zeros((ROWS, 256), F32)
            for k in range(TOPK):
                same = info[:, k : k + 1] == lane_expert
                match = jnp.where(same, 1.0, match)
                gates = jnp.where(same, info[:, TOPK + k : TOPK + k + 1], gates)
            earlier = dot(lower, match.astype(BF))
            here = jnp.where((earlier == lane_slot) & (lane_place == j), match, 0.0)
            none = jnp.zeros((ROWS, 256), F32)
            PTL[h, j] = jnp.concatenate([here, none], axis=0).astype(BF)
            PTR[h, j] = jnp.concatenate([none, here], axis=0).astype(BF)
            return total + jnp.sum(here * gates, axis=0, keepdims=True)

        total = lax.fori_loop(0, 8, slots_of, jnp.zeros((1, 256), F32))
        GM[:, 256 * h : 256 * h + 256] = jnp.broadcast_to(total, (8, 256))
    GS[me] = GM[...]
    moved_g = [remote(GM, GS.at[me], at_y(k)) for k in range(1, 8)]
    for h in range(2):
        PL[h] = jnp.transpose(PTL[h].reshape(8 * CH, 256).astype(F32)).astype(BF)
        PR[h] = jnp.transpose(PTR[h].reshape(8 * CH, 256).astype(F32)).astype(BF)

    for k in (1, 3, 2):
        moved_a[k].wait_recv()
    gain = pn_ref[:, x_cols(0)]
    stream = res_ref[:, x_cols(0)].astype(F32) + ((AP[0] + AR[0]) + (AR[1] + AR[2]))
    SM[...] = jnp.concatenate([stream[:, :CW], stream[:, CW:]], axis=0)
    scaled = stream * gain
    G[0] = jnp.concatenate([scaled[:, :CW], scaled[:, CW:]], axis=0).astype(BF)
    rows_z = direct(G)

    for copy in moved_g:
        copy.wait_recv()
    parts = []
    from_all = GS[:, 0, :]
    for h in range(2):
        part = jnp.zeros((8, 32), F32)
        for d in range(8):
            part = part + jnp.where(me == d, from_all[:, 256 * h + 32 * d : 256 * h + 32 * d + 32], 0.0)
        parts.append(part)
    slot_gate = jnp.concatenate(parts + [jnp.zeros((8, 64), F32)], axis=1)
    taken = (slot_gate > 0.0).astype(F32)
    taken16 = taken.astype(BF)

    def fields(dim):
        at = iota((128, 128), dim)
        nth = (at // 32) * 8 + (at // 2) % 8
        far = (nth + 1) // 2
        place = (z + jnp.where(nth % 2 == 1, -far, far) + 16) % 16
        return (at // 16) % 2, place, at % 2

    p_from, z_from, s_from = fields(0)
    p_to, z_to, s_to = fields(1)
    same_p = p_from == p_to
    before_z = (same_p & (z_from < z_to)).astype(F32).astype(BF)
    same_z = (same_p & (z_from == z_to)).astype(F32).astype(BF)
    before_s = (same_p & (z_from == z_to) & (s_from < s_to)).astype(F32).astype(BF)
    before_d = (iota((8, 8), 0) > iota((8, 8), 1)).astype(F32).astype(BF)
    ones = jnp.ones((8, 8), BF)
    rank = (
        dot(dot(ones, taken16).astype(BF), before_z)
        + dot(dot(before_d, taken16).astype(BF), same_z)
        + dot(taken16, before_s)
    )
    limit_0 = cap_ref[2 * row].astype(F32)
    limit_1 = cap_ref[2 * row + 1].astype(F32)
    limit = jnp.where((iota((8, 128), 1) // 16) % 2 == 0, limit_0, limit_1)
    kept = jnp.where(rank < limit, slot_gate, 0.0)
    kept_t = jnp.transpose(jnp.concatenate([kept] * 16, axis=0))
    for h in range(2):
        for p in range(2):
            at = (2 * h + p) * 16
            column = jnp.concatenate([kept_t[at : at + 16, d : d + 1] for d in range(8)], axis=0)
            KW[h, p] = jnp.broadcast_to(column, (128, 128))

    for via in (-1, 1, -3, 3, 5, -6):
        relay(G, rows_z, via)

    moved_y = []

    def select(h):
        for delta in ORDER[8 * h : 8 * h + 8]:
            if delta and delta not in RELAY.values():
                rows_z[delta].wait_recv()
        chunks = G[8 * h : 8 * h + 8].reshape(8 * CH, CW)
        S[h, :, :, :, 0:CW] = dot(PL[h], chunks).astype(BF).reshape(8, 2, 16, CW)
        S[h, :, :, :, CW:DX] = dot(PR[h], chunks).astype(BF).reshape(8, 2, 16, CW)
        moved_y.append([remote(S.at[h, ds[k]], R.at[h, :, me], at_y(k)) for k in range(1, 8)])
        for p in range(2):
            R[h, p, me] = S[h, me, p]

    moved_m = []

    def products(h):
        for copy in moved_y[h]:
            copy.wait_recv()
        for p in range(2):
            block = R[h, p].reshape(128, DX)
            for t in range(2):
                MS[h, 2 * p + t] = dot(block, W[2 * p + t]).astype(BF)
            plain = block.astype(F32) / gain
            squares = jnp.sum(plain * plain, axis=1, keepdims=True)
            SSB[h, p] = jnp.transpose(jnp.broadcast_to(squares, (128, 128)))[0:8]
        moved = []
        for k in (2, 1, 3):
            moved.append(remote(MS.at[h, xs[k]], MR.at[h, k - 1], at_x(k)))
            moved.append(remote(SSB.at[h, xs[k] // 2], SSR.at[h, k - 1], at_x(k)))
        moved_m.append(moved)

    moved_i = []

    def activate(h):
        for copy in moved_m[h]:
            copy.wait_recv()
        both = (MS[h, x].astype(F32) + MR[h, 0].astype(F32)) + (MR[h, 1].astype(F32) + MR[h, 2].astype(F32))
        squares = (SSB[h, x // 2] + SSR[h, 0]) + (SSR[h, 1] + SSR[h, 2])
        squares = jnp.transpose(jnp.concatenate([squares] * 16, axis=0))[:, 0:1]
        scale = lax.rsqrt(squares * (1.0 / 2048.0) + 1e-06)
        gate = both[:, 0:128] * scale
        up = both[:, 128:256] * scale
        IN[h, x] = (gate * sigmoid(gate) * up).astype(BF)
        moved_i.append([remote(IN.at[h, x], IN.at[h, x], at_x(k)) for k in (2, 1, 3)])

    moved_r = []

    def down(h):
        for copy in moved_i[h]:
            copy.wait_recv()
        for p in range(2):
            inner = jnp.concatenate([IN[h, 2 * p], IN[h, 2 * p + 1]], axis=1)
            part = dot(inner, D[2 * p : 2 * p + 2].reshape(256, DX))
            weight = KW[h, p]
            part = part * jnp.concatenate([weight] * 4, axis=1)
            Y[h, :, p] = part.astype(BF).reshape(8, 16, DX)
        moved_r.append([remote(Y.at[h, ds[k]], R2.at[h, me], at_y(k)) for k in range(1, 8)])
        R2[h, me] = Y[h, me]

    def combine(h):
        for copy in moved_r[h]:
            copy.wait_recv()
        back = R2[h].reshape(256, DX)
        left = dot(PTL[h].reshape(8 * CH, 256), back[:, 0:CW])
        right = dot(PTR[h].reshape(8 * CH, 256), back[:, CW:DX])
        C[8 * h : 8 * h + 8] = (left + right).reshape(8, CH, CW)

    select(0)
    select(1)
    for copy in own_w:
        copy.wait()
    for copy in moved_w:
        copy.wait_recv()
    products(0)
    products(1)
    activate(0)
    activate(1)
    down(0)
    down(1)
    combine(0)
    combine(1)

    back_z = {}

    def give(delta, via):
        place = PLACE[delta]
        back_z[delta] = remote(CB.at[place], T.at[place], at_z(delta - via))

    for delta, via in RELAY.items():
        CB[PLACE[delta]] = C[PLACE[delta]].astype(BF)
    for delta in (-8, -7, 7, 6, -5, -4, 4, -2, 2):
        give(delta, RELAY[delta])
    for via in (-1, 1, 3, -3, 5, -6):
        total = C[PLACE[via]]
        for delta, v in RELAY.items():
            if v == via:
                back_z[delta].wait_recv()
                total = total + T[PLACE[delta]].astype(F32)
        CB[PLACE[via]] = total.astype(BF)
        give(via, 0)
    mixed = SM[...] + C[0]
    for via in (-1, 1, 3, -3, 5, -6):
        back_z[via].wait_recv()
        mixed = mixed + T[PLACE[via]].astype(F32)

    mixed = jnp.concatenate([mixed[0:ROWS], mixed[ROWS:CH]], axis=1)
    for k in range(4):
        FX[k] = jnp.concatenate([mixed[6 * k : 6 * k + 6], jnp.zeros((2, DX), F32)], axis=0)
    FO[x] = FX[x]
    last = [remote(FX.at[xs[k]], FO.at[x], at_x(k)) for k in (2, 1, 3)]
    for copy in last:
        copy.wait_recv()
    for k in range(4):
        out_ref[:, DX * k : DX * k + DX] = FO[k, 0:6].astype(BF)
    for copy in sent:
        copy.wait_send()


def on_device(
    residual, queries, keys, values, out_gate, decay_input, beta_input, decay_log, decay_bias, past_state,
    head_norm, out_proj, post_norm, expert_ids, expert_gates, capacity, gate_proj, up_proj, down_proj,
):
    vmem = pl.BlockSpec(memory_space=pltpu.VMEM)
    smem = pl.BlockSpec(memory_space=pltpu.SMEM)
    hbm = pl.BlockSpec(memory_space=pl.ANY)
    scratch = [
        pltpu.VMEM((ROWS, HEADS, 128, 128), BF),
        pltpu.VMEM((4, DX, DX), BF),
        pltpu.VMEM((4, DX, 256), BF),
        pltpu.VMEM((4, 128, DX), BF),
        pltpu.VMEM((16, ROWS, 128), F32),
        pltpu.VMEM((2, 8 * ROWS, 128), F32),
        pltpu.VMEM((HEADS, 8 * ROWS, 128), F32),
        pltpu.VMEM((4, ROWS, DX), F32),
        pltpu.VMEM((3, ROWS, DX), F32),
        pltpu.VMEM((CH, CW), F32),
        pltpu.VMEM((16, CH, CW), BF),
        pltpu.VMEM((2, 8, CH, 256), BF),
        pltpu.VMEM((2, 8, CH, 256), BF),
        pltpu.VMEM((2, 256, 8 * CH), BF),
        pltpu.VMEM((2, 256, 8 * CH), BF),
        pltpu.VMEM((2, 8, 2, 16, DX), BF),
        pltpu.VMEM((2, 2, 8, 16, DX), BF),
        pltpu.VMEM((8, 512), F32),
        pltpu.VMEM((8, 8, 512), F32),
        pltpu.VMEM((2, 2, 128, 128), F32),
        pltpu.VMEM((2, 4, 128, 256), BF),
        pltpu.VMEM((2, 3, 128, 256), BF),
        pltpu.VMEM((2, 2, 8, 128), F32),
        pltpu.VMEM((2, 3, 8, 128), F32),
        pltpu.VMEM((2, 4, 128, 128), BF),
        pltpu.VMEM((2, 8, 2, 16, DX), BF),
        pltpu.VMEM((2, 8, 2, 16, DX), BF),
        pltpu.VMEM((16, CH, CW), F32),
        pltpu.VMEM((16, CH, CW), BF),
        pltpu.VMEM((16, CH, CW), BF),
        pltpu.VMEM((4, 8, DX), F32),
        pltpu.VMEM((4, 8, DX), F32),
        pltpu.SemaphoreType.DMA((N_SEM,)),
        pltpu.SemaphoreType.DMA((N_SEM,)),
        pltpu.SemaphoreType.DMA((16,)),
    ]
    return pl.pallas_call(
        kernel,
        out_shape=jax.ShapeDtypeStruct((6, 2048), BF),
        in_specs=[vmem] * 13 + [smem] + [hbm] * 5,
        out_specs=vmem,
        scratch_shapes=scratch,
        compiler_params=pltpu.CompilerParams(
            collective_id=1, has_side_effects=True, vmem_limit_bytes=40 * 1024 * 1024
        ),
        name="layer",
    )(
        residual, queries, keys, values, out_gate, decay_input, beta_input, decay_log[None, :], decay_bias[None, :],
        head_norm[None, :], post_norm[None, :], expert_ids, expert_gates, capacity,
        past_state, out_proj, gate_proj, up_proj, down_proj,
    )


def solution(mesh):
    placed = (
        P("row", None),
        P("row", "head"),
        P("row", "head"),
        P("row", "head"),
        P("row", "head"),
        P("row", "head"),
        P("row", "head"),
        P("head"),
        P("head"),
        P("row", "head", None, None),
        P(),
        P("head", None),
        P(),
        P("row", None),
        P("row", None),
        P(),
        P("row", None, "head"),
        P("row", None, "head"),
        P("row", "head", None),
    )
    return jax.shard_map(
        on_device, mesh=mesh, in_specs=placed, out_specs=P(("row", "head"), None), check_vma=False
    )
```

```python
import jax
import jax.numpy as jnp
from jax import lax
from jax.experimental import pallas as pl
from jax.experimental.pallas import tpu as pltpu
from jax.sharding import PartitionSpec as P

MESH = pl.DeviceIdType.MESH
BF = jnp.bfloat16
F32 = jnp.float32
HIGH = lax.Precision.HIGHEST

ROWS = 24
TOPK = 10
HEADS = 4
DX = 512
CH, CW = 48, 256
STEP = 4

ORDER = (0, -1, 1, -2, 2, -3, 3, -4, 4, -5, 5, -6, 6, -7, 7, -8)
PLACE = {delta: place for place, delta in enumerate(ORDER)}
DIRECT = (-6, 5, -3, 3, -1, 1)
RELAY = {-2: -1, 2: 1, -4: -3, -5: -3, 4: 3, 6: 5, 7: 5, -7: -6, -8: -6}
REACH = (-6, -5, -3, -2, -1, 1, 2, 3, 5, 6)
LEAVES = ((-4, -2, 2), (-8, -7, 7, 6, -5, 4))
N_SEM = 128
GATE_AT, DECAY_AT, BETA_AT = 16, 32, 40


def dot(a, b):
    return jnp.dot(a, b, preferred_element_type=F32)


def iota(shape, dim):
    return lax.broadcasted_iota(jnp.int32, shape, dim)


def sigmoid(v):
    return 1.0 / (1.0 + jnp.exp(-v))


def kernel(
    res_hbm, q_hbm, k_hbm, v_hbm, og_hbm, di_hbm, bi_hbm, dl_hbm, db_hbm, hn_hbm, pn_hbm,
    ids_hbm, eg_hbm, cap_hbm, state_hbm, op_hbm, gp_hbm, up_hbm, dp_hbm,
    out_ref,
    res_ref, q_ref, k_ref, v_ref, og_ref, di_ref, bi_ref, dl_ref, db_ref, hn_ref, pn_ref, ids_ref, eg_ref, cap_ref,
    NT,
    ST, OP, W, D, MG, AQ, RD, AP, AR, SM, G, PTL, PTR, PL, PR, S, R, MT, GT, GM, GS, KW,
    MS, MR, SSB, SSR, IN, Y, R2, C, CB, T, FX, FO,
    ss, rs, ls,
):
    row = lax.axis_index("row")
    x = lax.axis_index("head")
    z = row // 8
    me = row % 8
    xs = [x] + [(x + k) % 4 for k in range(1, 4)]
    ds = [me] + [(me + k) % 8 for k in range(1, 8)]

    def at_z(off):
        return (((z + 16 + off) % 16) * 8 + me, x)

    def at_y(k):
        return (z * 8 + ds[k], x)

    def at_x(k):
        return (row, xs[k])

    sent = []

    def remote(src, dst, device):
        n = len(sent)
        copy = pltpu.make_async_remote_copy(
            src_ref=src, dst_ref=dst, send_sem=ss.at[n], recv_sem=rs.at[n], device_id=device, device_id_type=MESH
        )
        copy.start()
        sent.append(copy)
        return copy

    n_local = [0]

    def local(src, dst):
        copy = pltpu.make_async_copy(src, dst, ls.at[n_local[0]])
        n_local[0] += 1
        copy.start()
        return copy

    def x_cols(k):
        return pl.ds(pl.multiple_of(xs[k] * DX, DX), DX)

    barrier = pltpu.get_barrier_semaphore()
    peers = [at_z(off) for off in REACH] + [at_y(k) for k in range(1, 8)] + [at_x(k) for k in range(1, 4)]
    for device in peers:
        pl.semaphore_signal(barrier, inc=1, device_id=device, device_id_type=MESH)

    lists = [local(ids_hbm, ids_ref), local(eg_hbm, eg_ref), local(di_hbm, di_ref), local(bi_hbm, bi_ref)]
    heads = [
        local(a, b)
        for a, b in (
            (q_hbm, q_ref), (k_hbm, k_ref), (v_hbm, v_ref), (og_hbm, og_ref), (dl_hbm, dl_ref), (db_hbm, db_ref),
            (hn_hbm, hn_ref),
        )
    ]
    states = [local(state_hbm.at[pl.ds(STEP * i, STEP)], ST.at[pl.ds(STEP * i, STEP)]) for i in range(ROWS // STEP)]
    later = [local(cap_hbm, cap_ref), local(res_hbm.at[:, x_cols(0)], res_ref), local(pn_hbm.at[:, x_cols(0)], pn_ref)]
    projs = [local(op_hbm.at[:, x_cols(k)], OP.at[k]) for k in (2, 1, 3, 0)]
    own_w = [
        local(gp_hbm.at[0, x_cols(0), :], W.at[x, :, pl.ds(0, 128)]),
        local(up_hbm.at[0, x_cols(0), :], W.at[x, :, pl.ds(128, 128)]),
        local(dp_hbm.at[0, :, x_cols(0)], D.at[x]),
    ]

    for copy in lists:
        copy.wait()
    NT[...] = jnp.zeros((128, 128), F32)
    NT[0:TOPK, 0:ROWS] = ids_ref[...].astype(F32)
    NT[GATE_AT : GATE_AT + TOPK, 0:ROWS] = eg_ref[...]
    NT[DECAY_AT : DECAY_AT + HEADS, 0:ROWS] = di_ref[...]
    NT[BETA_AT : BETA_AT + HEADS, 0:ROWS] = bi_ref[...]
    MG[0] = jnp.transpose(NT[...])[0:ROWS]
    pl.semaphore_wait(barrier, len(peers))

    def direct(buf):
        return {a: remote(buf.at[0], buf.at[PLACE[a]], at_z(-a)) for a in DIRECT}

    def relay(buf, copies, via):
        copies[via].wait_recv()
        for delta, v in RELAY.items():
            if v == via:
                copies[delta] = remote(buf.at[PLACE[v]], buf.at[PLACE[delta]], at_z(v - delta))

    meta = direct(MG)

    moved_w = [remote(gp_hbm.at[0, x_cols(k), :], W.at[x, :, pl.ds(0, 128)], at_x(k)) for k in (1, 3)]

    for copy in heads:
        copy.wait()
    narrow = MG[0]
    q_unit, k_unit, cross = [], [], []
    for g in range(2):
        for ref, scale, units, base in ((q_ref, 128 ** (-0.5), q_unit, 0), (k_ref, 1.0, k_unit, 2)):
            block = ref[:, 128 * g : 128 * g + 128].astype(F32)
            unit = block * (lax.rsqrt(jnp.sum(block * block, axis=1, keepdims=True) + 1e-06) * scale)
            high = unit.astype(BF).astype(F32)
            AQ[g, pl.ds(base, ROWS, stride=8), :] = high
            AQ[g, pl.ds(base + 1, ROWS, stride=8), :] = unit - high
            units.append(unit)
        for spare in range(4, 8):
            AQ[g, pl.ds(spare, ROWS, stride=8), :] = jnp.zeros((ROWS, 128), F32)
        cross.append(jnp.sum(q_unit[g] * k_unit[g], axis=1, keepdims=True))

    def read_rows(i):
        for u in range(STEP):
            r = STEP * i + u
            at = pl.ds(pl.multiple_of(r * 8, 8), 8)
            for g in range(2):
                a = AQ[g, at, :].astype(BF)
                for h in (2 * g, 2 * g + 1):
                    RD[h, at, :] = dot(a, ST[r, h])

    for copy in states:
        copy.wait()
    pl.loop(0, ROWS // STEP)(read_rows)

    gated = []
    for h in range(HEADS):
        g = h // 2
        read_q = RD[h, pl.ds(0, ROWS, stride=8), :] + RD[h, pl.ds(1, ROWS, stride=8), :]
        read_k = RD[h, pl.ds(2, ROWS, stride=8), :] + RD[h, pl.ds(3, ROWS, stride=8), :]
        arg = narrow[:, DECAY_AT + h : DECAY_AT + h + 1] + db_ref[:, h : h + 1]
        soft = jnp.maximum(arg, 0.0) + jnp.log(1.0 + jnp.exp(-jnp.abs(arg)))
        decay = jnp.exp(-jnp.exp(dl_ref[:, h : h + 1]) * soft)
        beta = sigmoid(narrow[:, BETA_AT + h : BETA_AT + h + 1])
        cols = slice(128 * h, 128 * h + 128)
        update = beta * (v_ref[:, cols].astype(F32) - decay * read_k)
        head_out = decay * read_q + cross[g] * update
        norm = head_out * lax.rsqrt(jnp.mean(head_out * head_out, axis=1, keepdims=True) + 1e-06) * hn_ref[...]
        gate = og_ref[:, cols].astype(F32)
        gated.append((norm * (gate * sigmoid(gate))).astype(BF))
    gated = jnp.concatenate(gated, axis=1)

    moved_a = {}
    for copy, k in zip(projs, (2, 1, 3, 0)):
        copy.wait()
        AP[k] = dot(gated, OP[k])
        if k:
            moved_a[k] = remote(AP.at[k], AR.at[k - 1], at_x(k))

    for via in (-1, 1, -3, 3):
        relay(MG, meta, via)

    for k in (1, 3, 2):
        moved_a[k].wait_recv()
    for copy in later:
        copy.wait()
    gain = pn_ref[...]
    inverse = 1.0 / gain
    stream = res_ref[...].astype(F32) + ((AP[0] + AR[0]) + (AR[1] + AR[2]))
    SM[...] = jnp.concatenate([stream[:, :CW], stream[:, CW:]], axis=0)
    scaled = stream * gain
    G[0] = jnp.concatenate([scaled[:, :CW], scaled[:, CW:]], axis=0).astype(BF)
    rows_z = direct(G)
    moved_w.append(remote(gp_hbm.at[0, x_cols(2), :], W.at[x, :, pl.ds(0, 128)], at_x(2)))
    for k in (2, 1, 3):
        moved_w.append(remote(up_hbm.at[0, x_cols(k), :], W.at[x, :, pl.ds(128, 128)], at_x(k)))
    moved_d = [remote(dp_hbm.at[0, :, x_cols(k)], D.at[x], at_x(k)) for k in (2, 1, 3)]

    for via in (5, -6):
        relay(MG, meta, via)
    for delta in RELAY:
        meta[delta].wait_recv()
    lane = iota((ROWS, 128), 1)
    lane_expert = jnp.where(lane < 32, 16 * z + lane // 2, -1).astype(F32)

    def name_slots(i):
        for u in range(4):
            j = 4 * i + u
            info = MG[j]
            match = jnp.zeros((ROWS, 128), F32)
            gates = jnp.zeros((ROWS, 128), F32)
            for k in range(TOPK):
                same = info[:, k : k + 1] == lane_expert
                match = jnp.where(same, 1.0, match)
                gates = jnp.where(same, info[:, GATE_AT + k : GATE_AT + k + 1], gates)
            at = pl.ds(pl.multiple_of(j * ROWS, 8), ROWS)
            MT[at, :] = match
            GT[at, :] = gates

    pl.loop(0, 4)(name_slots)
    half = 8 * ROWS
    row_a, row_b = iota((half, half), 0), iota((half, half), 1)
    lower = ((row_a > row_b) & (row_a // ROWS == row_b // ROWS)).astype(F32).astype(BF)
    spread = (
        (iota((128, 256), 0) // 2 == iota((128, 256), 1) // 16)
        & (iota((128, 256), 0) % 2 == (iota((128, 256), 1) // 8) % 2)
    )
    spread = spread.astype(F32).astype(BF)
    lane_slot = (iota((half, 128), 1) % 2).astype(F32)
    lane_place = iota((half, 256), 1) % 8
    def place_slots(h):
        match = MT[half * h : half * h + half, :]
        earlier = dot(lower, match.astype(BF))
        here = jnp.where(earlier == lane_slot, match, 0.0)
        gates = here * GT[half * h : half * h + half, :]
        GM[8 * h : 8 * h + 8, :] = jnp.concatenate(
            [jnp.sum(gates[ROWS * j : ROWS * j + ROWS], axis=0, keepdims=True) for j in range(8)], axis=0
        )
        placed = jnp.where(lane_place == iota((half, 256), 0) // ROWS, dot(here.astype(BF), spread), 0.0)
        none = jnp.zeros((ROWS, 256), F32)
        for j in range(8):
            one = placed[ROWS * j : ROWS * j + ROWS]
            PTL[h, j] = jnp.concatenate([one, none], axis=0).astype(BF)
            PTR[h, j] = jnp.concatenate([none, one], axis=0).astype(BF)
        PL[h] = jnp.transpose(PTL[h].reshape(8 * CH, 256).astype(F32)).astype(BF)
        PR[h] = jnp.transpose(PTR[h].reshape(8 * CH, 256).astype(F32)).astype(BF)

    moved_y = []

    def select(h):
        for delta in ORDER[8 * h : 8 * h + 8]:
            if delta and delta not in RELAY.values():
                rows_z[delta].wait_recv()
        chunks = G[8 * h : 8 * h + 8].reshape(8 * CH, CW)
        S[h, :, :, :, 0:CW] = dot(PL[h], chunks).astype(BF).reshape(8, 2, 16, CW)
        S[h, :, :, :, CW:DX] = dot(PR[h], chunks).astype(BF).reshape(8, 2, 16, CW)
        moved_y.append([remote(S.at[h, ds[k]], R.at[h, :, me], at_y(k)) for k in range(1, 8)])
        for p in range(2):
            R[h, p, me] = S[h, me, p]

    moved_m = []

    def products(h):
        for copy in moved_y[h]:
            copy.wait_recv()
        for p in range(2):
            block = R[h, p].reshape(128, DX)
            for t in range(2):
                MS[h, 2 * p + t] = dot(block, W[2 * p + t]).astype(BF)
            plain = block.astype(F32) * inverse
            squares = jnp.sum(plain * plain, axis=1, keepdims=True)
            SSB[h, p] = jnp.transpose(jnp.broadcast_to(squares, (128, 128)))[0:8]
        moved = []
        for k in (2, 1, 3):
            moved.append(remote(MS.at[h, xs[k]], MR.at[h, k - 1], at_x(k)))
            moved.append(remote(SSB.at[h, xs[k] // 2], SSR.at[h, k - 1], at_x(k)))
        moved_m.append(moved)

    moved_i = []

    def activate(h):
        for copy in moved_m[h]:
            copy.wait_recv()
        both = (MS[h, x].astype(F32) + MR[h, 0].astype(F32)) + (MR[h, 1].astype(F32) + MR[h, 2].astype(F32))
        squares = (SSB[h, x // 2] + SSR[h, 0]) + (SSR[h, 1] + SSR[h, 2])
        squares = jnp.transpose(jnp.concatenate([squares] * 16, axis=0))[:, 0:1]
        scale = lax.rsqrt(squares * (1.0 / 2048.0) + 1e-06)
        gate = both[:, 0:128] * scale
        up = both[:, 128:256] * scale
        IN[h, x] = (gate * sigmoid(gate) * up).astype(BF)
        moved_i.append([remote(IN.at[h, x], IN.at[h, x], at_x(k)) for k in (2, 1, 3)])

    moved_r = []

    def down(h):
        if h == 0:
            for copy in moved_d:
                copy.wait_recv()
        for copy in moved_i[h]:
            copy.wait_recv()
        for p in range(2):
            inner = jnp.concatenate([IN[h, 2 * p], IN[h, 2 * p + 1]], axis=1)
            part = dot(inner, D[2 * p : 2 * p + 2].reshape(256, DX))
            weight = KW[h, p]
            part = part * jnp.concatenate([weight] * 4, axis=1)
            Y[h, :, p] = part.astype(BF).reshape(8, 16, DX)
        moved_r.append([remote(Y.at[h, ds[k]], R2.at[h, me], at_y(k)) for k in range(1, 8)])
        R2[h, me] = Y[h, me]

    def combine(h):
        for copy in moved_r[h]:
            copy.wait_recv()
        back = R2[h].reshape(256, DX)
        left = dot(PTL[h].reshape(8 * CH, 256), back[:, 0:CW])
        right = dot(PTR[h].reshape(8 * CH, 256), back[:, CW:DX])
        C[8 * h : 8 * h + 8] = (left + right).reshape(8, CH, CW)

    back_z = {}

    def give(delta, via):
        place = PLACE[delta]
        back_z[delta] = remote(CB.at[place], T.at[place], at_z(delta - via))

    def leaves(h):
        for delta in LEAVES[h]:
            CB[PLACE[delta]] = C[PLACE[delta]].astype(BF)
            give(delta, RELAY[delta])

    def weigh():
        for copy in moved_g:
            copy.wait_recv()
        slot_gate = GS[...].reshape(128, 128)
        taken = (slot_gate > 0.0).astype(F32).astype(BF)

        def order(dim):
            at = iota((128, 128), dim)
            nth = at % 16
            far = (nth + 1) // 2
            place = (z + jnp.where(nth % 2 == 1, -far, far) + 16) % 16
            return place * 8 + at // 16

        before = (order(1) < order(0)).astype(F32).astype(BF)
        lane_a, lane_b = iota((128, 128), 0), iota((128, 128), 1)
        pair = (lane_a // 2 == lane_b // 2).astype(F32).astype(BF)
        first = ((lane_a // 2 == lane_b // 2) & (lane_a < lane_b)).astype(F32).astype(BF)
        rank = dot(before, dot(taken, pair).astype(BF)) + dot(taken, first)
        limit_0 = cap_ref[2 * row].astype(F32)
        limit_1 = cap_ref[2 * row + 1].astype(F32)
        limit = jnp.where((lane_b // 2) % 2 == 0, limit_0, limit_1)
        kept = jnp.where(rank < limit, slot_gate, 0.0)
        for p in range(2):
            columns = [
                jnp.sum(jnp.where(lane_b == 4 * me + 2 * p + t, kept, 0.0), axis=1, keepdims=True) for t in range(2)
            ]
            for h in range(2):
                column = jnp.concatenate(
                    [c[16 * d + 8 * h : 16 * d + 8 * h + 8] for d in range(8) for c in columns], axis=0
                )
                KW[h, p] = jnp.broadcast_to(column, (128, 128))

    for via in (-1, 1, -3, 3):
        relay(G, rows_z, via)
    place_slots(0)
    for via in (5, -6):
        relay(G, rows_z, via)
    select(0)
    place_slots(1)
    select(1)
    GS[me] = GM[...]
    moved_g = [remote(GM, GS.at[me], at_y(k)) for k in range(1, 8)]

    for copy in own_w:
        copy.wait()
    for copy in moved_w:
        copy.wait_recv()
    products(0)
    products(1)
    activate(0)
    weigh()
    activate(1)
    down(0)
    down(1)
    combine(0)
    leaves(0)
    combine(1)
    leaves(1)

    for via in (-6, 5, -3, 3, -1, 1):
        total = C[PLACE[via]]
        for delta, v in RELAY.items():
            if v == via:
                back_z[delta].wait_recv()
                total = total + T[PLACE[delta]].astype(F32)
        CB[PLACE[via]] = total.astype(BF)
        give(via, 0)
    mixed = SM[...] + C[0]
    for via in (-1, 1, 3, -3, 5, -6):
        back_z[via].wait_recv()
        mixed = mixed + T[PLACE[via]].astype(F32)

    mixed = jnp.concatenate([mixed[0:ROWS], mixed[ROWS:CH]], axis=1)
    for k in range(4):
        FX[k] = jnp.concatenate([mixed[6 * k : 6 * k + 6], jnp.zeros((2, DX), F32)], axis=0)
    FO[x] = FX[x]
    last = [remote(FX.at[xs[k]], FO.at[x], at_x(k)) for k in (2, 1, 3)]
    for copy in last:
        copy.wait_recv()
    for k in range(4):
        out_ref[:, DX * k : DX * k + DX] = FO[k, 0:6].astype(BF)
    for copy in sent:
        copy.wait_send()


def on_device(
    residual, queries, keys, values, out_gate, decay_input, beta_input, decay_log, decay_bias, past_state,
    head_norm, out_proj, post_norm, expert_ids, expert_gates, capacity, gate_proj, up_proj, down_proj,
):
    vmem = pl.BlockSpec(memory_space=pltpu.VMEM)
    hbm = pl.BlockSpec(memory_space=pl.ANY)
    scratch = [
        pltpu.VMEM((ROWS, DX), BF),
        pltpu.VMEM((ROWS, 256), BF),
        pltpu.VMEM((ROWS, 256), BF),
        pltpu.VMEM((ROWS, DX), BF),
        pltpu.VMEM((ROWS, DX), BF),
        pltpu.VMEM((HEADS, ROWS), F32),
        pltpu.VMEM((HEADS, ROWS), F32),
        pltpu.VMEM((1, HEADS), F32),
        pltpu.VMEM((1, HEADS), F32),
        pltpu.VMEM((1, 128), F32),
        pltpu.VMEM((1, DX), F32),
        pltpu.VMEM((TOPK, ROWS), jnp.int32),
        pltpu.VMEM((TOPK, ROWS), F32),
        pltpu.SMEM((256,), jnp.int32),
        pltpu.VMEM((128, 128), F32),
        pltpu.VMEM((ROWS, HEADS, 128, 128), BF),
        pltpu.VMEM((4, DX, DX), BF),
        pltpu.VMEM((4, DX, 256), BF),
        pltpu.VMEM((4, 128, DX), BF),
        pltpu.VMEM((16, ROWS, 128), F32),
        pltpu.VMEM((2, 8 * ROWS, 128), F32),
        pltpu.VMEM((HEADS, 8 * ROWS, 128), F32),
        pltpu.VMEM((4, ROWS, DX), F32),
        pltpu.VMEM((3, ROWS, DX), F32),
        pltpu.VMEM((CH, CW), F32),
        pltpu.VMEM((16, CH, CW), BF),
        pltpu.VMEM((2, 8, CH, 256), BF),
        pltpu.VMEM((2, 8, CH, 256), BF),
        pltpu.VMEM((2, 256, 8 * CH), BF),
        pltpu.VMEM((2, 256, 8 * CH), BF),
        pltpu.VMEM((2, 8, 2, 16, DX), BF),
        pltpu.VMEM((2, 2, 8, 16, DX), BF),
        pltpu.VMEM((16 * ROWS, 128), F32),
        pltpu.VMEM((16 * ROWS, 128), F32),
        pltpu.VMEM((16, 128), F32),
        pltpu.VMEM((8, 16, 128), F32),
        pltpu.VMEM((2, 2, 128, 128), F32),
        pltpu.VMEM((2, 4, 128, 256), BF),
        pltpu.VMEM((2, 3, 128, 256), BF),
        pltpu.VMEM((2, 2, 8, 128), F32),
        pltpu.VMEM((2, 3, 8, 128), F32),
        pltpu.VMEM((2, 4, 128, 128), BF),
        pltpu.VMEM((2, 8, 2, 16, DX), BF),
        pltpu.VMEM((2, 8, 2, 16, DX), BF),
        pltpu.VMEM((16, CH, CW), F32),
        pltpu.VMEM((16, CH, CW), BF),
        pltpu.VMEM((16, CH, CW), BF),
        pltpu.VMEM((4, 8, DX), F32),
        pltpu.VMEM((4, 8, DX), F32),
        pltpu.SemaphoreType.DMA((N_SEM,)),
        pltpu.SemaphoreType.DMA((N_SEM,)),
        pltpu.SemaphoreType.DMA((32,)),
    ]
    return pl.pallas_call(
        kernel,
        out_shape=pltpu.VMEM((6, 2048), BF),
        in_specs=[hbm] * 19,
        out_specs=vmem,
        scratch_shapes=scratch,
        compiler_params=pltpu.CompilerParams(
            collective_id=1, has_side_effects=True, vmem_limit_bytes=60 * 1024 * 1024
        ),
        name="layer",
    )(
        *[pltpu.with_memory_space_constraint(array, pltpu.HBM) for array in (
        residual, queries, keys, values, out_gate, decay_input.T, beta_input.T, decay_log[None, :], decay_bias[None, :],
        head_norm[None, :], post_norm[None, :], expert_ids.T, expert_gates.T, capacity,
        past_state, out_proj, gate_proj, up_proj, down_proj,
        )]
    )


def solution(mesh):
    placed = (
        P("row", None),
        P("row", "head"),
        P("row", "head"),
        P("row", "head"),
        P("row", "head"),
        P("row", "head"),
        P("row", "head"),
        P("head"),
        P("head"),
        P("row", "head", None, None),
        P(),
        P("head", None),
        P(),
        P("row", None),
        P("row", None),
        P(),
        P("row", None, "head"),
        P("row", None, "head"),
        P("row", "head", None),
    )
    return jax.shard_map(
        on_device, mesh=mesh, in_specs=placed, out_specs=P(("row", "head"), None), check_vma=False
    )
```

```python
import jax
import jax.numpy as jnp
from jax import lax
from jax.experimental import pallas as pl
from jax.experimental.pallas import tpu as pltpu
from jax.sharding import PartitionSpec as P

MESH = pl.DeviceIdType.MESH
BF = jnp.bfloat16
F32 = jnp.float32
HIGH = lax.Precision.HIGHEST

ROWS = 24
TOPK = 10
HEADS = 4
DX = 512
CH, CW = 48, 256
STEP = 4

ORDER = (0, -1, 1, -2, 2, -3, 3, -4, 4, -5, 5, -6, 6, -7, 7, -8)
PLACE = {delta: place for place, delta in enumerate(ORDER)}
DIRECT = (-6, 5, -3, 3, -1, 1)
RELAY = {-2: -1, 2: 1, -4: -3, -5: -3, 4: 3, 6: 5, 7: 5, -7: -6, -8: -6}
REACH = (-6, -5, -3, -2, -1, 1, 2, 3, 5, 6)
BLOCKS = 4
LEAVES = ((-2,), (-4, 2), (-5, 4), (-8, -7, 7, 6))
N_SEM = 192
GATE_AT, DECAY_AT, BETA_AT = 16, 32, 40


def dot(a, b):
    return jnp.dot(a, b, preferred_element_type=F32)


def iota(shape, dim):
    return lax.broadcasted_iota(jnp.int32, shape, dim)


def sigmoid(v):
    return 1.0 / (1.0 + jnp.exp(-v))


def kernel(
    res_hbm, q_hbm, k_hbm, v_hbm, og_hbm, di_hbm, bi_hbm, dl_hbm, db_hbm, hn_hbm, pn_hbm,
    ids_hbm, eg_hbm, cap_hbm, state_hbm, op_hbm, gp_hbm, up_hbm, dp_hbm,
    out_ref,
    res_ref, q_ref, k_ref, v_ref, og_ref, di_ref, bi_ref, dl_ref, db_ref, hn_ref, pn_ref, ids_ref, eg_ref, cap_ref,
    NT,
    ST, OP, W, D, MG, AQ, RD, AP, AR, SM, G, PTL, PTR, PL, PR, S, R, MT, GT, GM, GS, KW,
    MS, MR, SSB, SSR, IN, Y, R2, C, CB, T, FX, FO,
    ss, rs, ls,
):
    row = lax.axis_index("row")
    x = lax.axis_index("head")
    z = row // 8
    me = row % 8
    xs = [x] + [(x + k) % 4 for k in range(1, 4)]
    ds = [me] + [(me + k) % 8 for k in range(1, 8)]

    def at_z(off):
        return (((z + 16 + off) % 16) * 8 + me, x)

    def at_y(k):
        return (z * 8 + ds[k], x)

    def at_x(k):
        return (row, xs[k])

    sent = []

    def remote(src, dst, device):
        n = len(sent)
        copy = pltpu.make_async_remote_copy(
            src_ref=src, dst_ref=dst, send_sem=ss.at[n], recv_sem=rs.at[n], device_id=device, device_id_type=MESH
        )
        copy.start()
        sent.append(copy)
        return copy

    n_local = [0]

    def local(src, dst):
        copy = pltpu.make_async_copy(src, dst, ls.at[n_local[0]])
        n_local[0] += 1
        copy.start()
        return copy

    def x_cols(k):
        return pl.ds(pl.multiple_of(xs[k] * DX, DX), DX)

    barrier = pltpu.get_barrier_semaphore()
    peers = [at_z(off) for off in REACH] + [at_y(k) for k in range(1, 8)] + [at_x(k) for k in range(1, 4)]
    for device in peers:
        pl.semaphore_signal(barrier, inc=1, device_id=device, device_id_type=MESH)

    lists = [local(ids_hbm, ids_ref), local(eg_hbm, eg_ref), local(di_hbm, di_ref), local(bi_hbm, bi_ref)]
    heads = [
        local(a, b)
        for a, b in (
            (q_hbm, q_ref), (k_hbm, k_ref), (v_hbm, v_ref), (og_hbm, og_ref), (dl_hbm, dl_ref), (db_hbm, db_ref),
            (hn_hbm, hn_ref),
        )
    ]
    states = [local(state_hbm.at[pl.ds(STEP * i, STEP)], ST.at[pl.ds(STEP * i, STEP)]) for i in range(ROWS // STEP)]
    later = [local(cap_hbm, cap_ref), local(res_hbm.at[:, x_cols(0)], res_ref), local(pn_hbm.at[:, x_cols(0)], pn_ref)]
    projs = [local(op_hbm.at[:, x_cols(k)], OP.at[k]) for k in (2, 1, 3, 0)]
    own_w = [
        local(gp_hbm.at[0, x_cols(0), :], W.at[x, :, pl.ds(0, 128)]),
        local(up_hbm.at[0, x_cols(0), :], W.at[x, :, pl.ds(128, 128)]),
        local(dp_hbm.at[0, :, x_cols(0)], D.at[x]),
    ]

    for copy in lists:
        copy.wait()
    NT[...] = jnp.zeros((128, 128), F32)
    NT[0:TOPK, 0:ROWS] = ids_ref[...].astype(F32)
    NT[GATE_AT : GATE_AT + TOPK, 0:ROWS] = eg_ref[...]
    NT[DECAY_AT : DECAY_AT + HEADS, 0:ROWS] = di_ref[...]
    NT[BETA_AT : BETA_AT + HEADS, 0:ROWS] = bi_ref[...]
    narrow = jnp.transpose(NT[...])[0:ROWS]
    MG[0] = jnp.concatenate([narrow[8 * g : 8 * g + 8, 0:32] for g in range(3)] + [jnp.zeros((8, 32), F32)], axis=1)
    pl.semaphore_wait(barrier, len(peers))

    def direct(buf):
        return {a: remote(buf.at[0], buf.at[PLACE[a]], at_z(-a)) for a in DIRECT}

    def relay(buf, copies, via):
        copies[via].wait_recv()
        for delta, v in RELAY.items():
            if v == via:
                copies[delta] = remote(buf.at[PLACE[v]], buf.at[PLACE[delta]], at_z(v - delta))

    meta = direct(MG)

    moved_w = [remote(gp_hbm.at[0, x_cols(k), :], W.at[x, :, pl.ds(0, 128)], at_x(k)) for k in (1, 3)]

    for copy in heads:
        copy.wait()
    q_unit, k_unit, cross = [], [], []
    for g in range(2):
        for ref, scale, units, base in ((q_ref, 128 ** (-0.5), q_unit, 0), (k_ref, 1.0, k_unit, 2)):
            block = ref[:, 128 * g : 128 * g + 128].astype(F32)
            unit = block * (lax.rsqrt(jnp.sum(block * block, axis=1, keepdims=True) + 1e-06) * scale)
            high = unit.astype(BF).astype(F32)
            AQ[g, pl.ds(base, ROWS, stride=8), :] = high
            AQ[g, pl.ds(base + 1, ROWS, stride=8), :] = unit - high
            units.append(unit)
        for spare in range(4, 8):
            AQ[g, pl.ds(spare, ROWS, stride=8), :] = jnp.zeros((ROWS, 128), F32)
        cross.append(jnp.sum(q_unit[g] * k_unit[g], axis=1, keepdims=True))

    def read_rows(i):
        for u in range(STEP):
            r = STEP * i + u
            at = pl.ds(pl.multiple_of(r * 8, 8), 8)
            for g in range(2):
                a = AQ[g, at, :].astype(BF)
                for h in (2 * g, 2 * g + 1):
                    RD[h, at, :] = dot(a, ST[r, h])

    for copy in states:
        copy.wait()
    pl.loop(0, ROWS // STEP)(read_rows)

    gated = []
    for h in range(HEADS):
        g = h // 2
        read_q = RD[h, pl.ds(0, ROWS, stride=8), :] + RD[h, pl.ds(1, ROWS, stride=8), :]
        read_k = RD[h, pl.ds(2, ROWS, stride=8), :] + RD[h, pl.ds(3, ROWS, stride=8), :]
        arg = narrow[:, DECAY_AT + h : DECAY_AT + h + 1] + db_ref[:, h : h + 1]
        soft = jnp.maximum(arg, 0.0) + jnp.log(1.0 + jnp.exp(-jnp.abs(arg)))
        decay = jnp.exp(-jnp.exp(dl_ref[:, h : h + 1]) * soft)
        beta = sigmoid(narrow[:, BETA_AT + h : BETA_AT + h + 1])
        cols = slice(128 * h, 128 * h + 128)
        update = beta * (v_ref[:, cols].astype(F32) - decay * read_k)
        head_out = decay * read_q + cross[g] * update
        norm = head_out * lax.rsqrt(jnp.mean(head_out * head_out, axis=1, keepdims=True) + 1e-06) * hn_ref[...]
        gate = og_ref[:, cols].astype(F32)
        gated.append((norm * (gate * sigmoid(gate))).astype(BF))
    gated = jnp.concatenate(gated, axis=1)

    moved_a = {}
    for copy, k in zip(projs, (2, 1, 3, 0)):
        copy.wait()
        AP[k] = dot(gated, OP[k])
        if k:
            moved_a[k] = remote(AP.at[k], AR.at[k - 1], at_x(k))

    for via in (-1, 1, -3, 3, 5, -6):
        relay(MG, meta, via)

    for k in (1, 3, 2):
        moved_a[k].wait_recv()
    for copy in later:
        copy.wait()
    gain = pn_ref[...]
    inverse = 1.0 / gain
    stream = res_ref[...].astype(F32) + ((AP[0] + AR[0]) + (AR[1] + AR[2]))
    SM[...] = jnp.concatenate([stream[:, :CW], stream[:, CW:]], axis=0)
    scaled = stream * gain
    G[0] = jnp.concatenate([scaled[:, :CW], scaled[:, CW:]], axis=0).astype(BF)
    rows_z = direct(G)
    moved_w.append(remote(gp_hbm.at[0, x_cols(2), :], W.at[x, :, pl.ds(0, 128)], at_x(2)))
    for k in (2, 1, 3):
        moved_w.append(remote(up_hbm.at[0, x_cols(k), :], W.at[x, :, pl.ds(128, 128)], at_x(k)))
    moved_d = [remote(dp_hbm.at[0, :, x_cols(k)], D.at[x], at_x(k)) for k in (2, 1, 3)]

    for via in (-1, 1):
        relay(G, rows_z, via)
    for delta in RELAY:
        meta[delta].wait_recv()
    lane = iota((ROWS, 128), 1)
    lane_expert = jnp.where(lane < 32, 16 * z + (lane >> 1), -1).astype(F32)[0:8]

    def name_slots(i):
        for u in range(4):
            j = 4 * i + u
            info = MG[j]
            for g in range(3):
                match = jnp.zeros((8, 128), F32)
                gates = jnp.zeros((8, 128), F32)
                for k in range(TOPK):
                    same = info[:, 32 * g + k : 32 * g + k + 1] == lane_expert
                    match = jnp.where(same, 1.0, match)
                    gates = jnp.where(same, info[:, 32 * g + GATE_AT + k : 32 * g + GATE_AT + k + 1], gates)
                at = pl.ds(pl.multiple_of(j * ROWS + 8 * g, 8), 8)
                MT[at, :] = match
                GT[at, :] = gates

    pl.loop(0, 4)(name_slots)
    later_row = (iota((ROWS, ROWS), 0) > iota((ROWS, ROWS), 1)).astype(F32).astype(BF)
    lane_c, lane_w = iota((128, 128), 0), iota((128, 128), 1)
    spread = ((lane_c >> 1) == (lane_w >> 3)) & ((lane_c & 1) == ((lane_w >> 2) & 1))
    spread = spread.astype(F32).astype(BF)
    lane_slot = (lane & 1).astype(F32)
    lane_place = lane & 3

    def place_slots(b):
        totals = []
        for u in range(4):
            at = slice(ROWS * (4 * b + u), ROWS * (4 * b + u) + ROWS)
            match = MT[at, :]
            here = jnp.where(dot(later_row, match.astype(BF)) == lane_slot, match, 0.0)
            totals.append(jnp.sum(here * GT[at, :], axis=0, keepdims=True))
            placed = jnp.where(lane_place == u, dot(here.astype(BF), spread), 0.0)
            none = jnp.zeros((ROWS, 128), F32)
            PTL[b, u] = jnp.concatenate([placed, none], axis=0).astype(BF)
            PTR[b, u] = jnp.concatenate([none, placed], axis=0).astype(BF)
        GM[8 * b : 8 * b + 8, :] = jnp.concatenate(totals * 2, axis=0)
        PL[b] = jnp.transpose(PTL[b].reshape(4 * CH, 128).astype(F32)).astype(BF)
        PR[b] = jnp.transpose(PTR[b].reshape(4 * CH, 128).astype(F32)).astype(BF)

    for via in (-3, 3):
        relay(G, rows_z, via)
    place_slots(0)
    for via in (5, -6):
        relay(G, rows_z, via)
    moved_y = []

    def select(b):
        for delta in ORDER[4 * b : 4 * b + 4]:
            if delta and delta not in RELAY.values():
                rows_z[delta].wait_recv()
        chunks = G[4 * b : 4 * b + 4].reshape(4 * CH, CW)
        S[b, :, :, 0:CW] = dot(PL[b], chunks).astype(BF).reshape(8, 16, CW)
        S[b, :, :, CW:DX] = dot(PR[b], chunks).astype(BF).reshape(8, 16, CW)
        moved_y.append([remote(S.at[b, ds[k]], R.at[b, me], at_y(k)) for k in (4, 5, 3, 2, 6, 7, 1)])
        R[b, me] = S[b, me]

    moved_m = []

    def products(b):
        for copy in moved_y[b]:
            copy.wait_recv()
        block = R[b].reshape(128, DX)
        for t in range(4):
            both = dot(block, W[t]).reshape(8, 2, 8, 256)[:, t // 2]
            MS[b, t] = both.reshape(64, 256).astype(BF)
        plain = block.astype(F32) * inverse
        squares = jnp.sum(plain * plain, axis=1, keepdims=True)
        SSB[b] = jnp.transpose(jnp.broadcast_to(squares, (128, 128)))[0:8]
        moved = []
        for k in (2, 1, 3):
            moved.append(remote(MS.at[b, xs[k]], MR.at[b, k - 1], at_x(k)))
            moved.append(remote(SSB.at[b], SSR.at[b, k - 1], at_x(k)))
        moved_m.append(moved)

    moved_i = []

    def activate(b):
        for copy in moved_m[b]:
            copy.wait_recv()
        both = (MS[b, x].astype(F32) + MR[b, 0].astype(F32)) + (MR[b, 1].astype(F32) + MR[b, 2].astype(F32))
        squares = (SSB[b] + SSR[b, 0]) + (SSR[b, 1] + SSR[b, 2])
        squares = jnp.transpose(jnp.concatenate([squares] * 16, axis=0))[:, 0:1].reshape(8, 2, 8, 1)
        squares = jnp.where(x // 2 == 0, squares[:, 0], squares[:, 1]).reshape(64, 1)
        scale = lax.rsqrt(squares * (1.0 / 2048.0) + 1e-06)
        gate = both[:, 0:128] * scale
        up = both[:, 128:256] * scale
        IN[b, x] = (gate * sigmoid(gate) * up).astype(BF)
        moved_i.append([remote(IN.at[b, x], IN.at[b, x], at_x(k)) for k in (2, 1, 3)])

    moved_r = []

    def down(b):
        if b == 0:
            for copy in moved_d:
                copy.wait_recv()
        for copy in moved_i[b]:
            copy.wait_recv()
        parts = []
        for p in range(2):
            inner = jnp.concatenate([IN[b, 2 * p], IN[b, 2 * p + 1]], axis=1)
            part = dot(inner, D[2 * p : 2 * p + 2].reshape(256, DX))
            part = part * jnp.concatenate([KW[b, p]] * 4, axis=1)
            parts.append(part.reshape(8, 8, DX))
        Y[b] = jnp.concatenate(parts, axis=1).astype(BF)
        moved_r.append([remote(Y.at[b, ds[k]], R2.at[b, me], at_y(k)) for k in (4, 5, 3, 2, 6, 7, 1)])
        R2[b, me] = Y[b, me]

    def combine(b):
        for copy in moved_r[b]:
            copy.wait_recv()
        back = R2[b].reshape(128, DX)
        left = dot(PTL[b].reshape(4 * CH, 128), back[:, 0:CW])
        right = dot(PTR[b].reshape(4 * CH, 128), back[:, CW:DX])
        C[4 * b : 4 * b + 4] = (left + right).reshape(4, CH, CW)

    back_z = {}

    def give(delta, via):
        place = PLACE[delta]
        back_z[delta] = remote(CB.at[place], T.at[place], at_z(delta - via))

    def leaves(b):
        for delta in LEAVES[b]:
            CB[PLACE[delta]] = C[PLACE[delta]].astype(BF)
            give(delta, RELAY[delta])

    def weigh():
        for copy in moved_g:
            copy.wait_recv()
        slot_gate = GS[...].reshape(256, 128)
        taken = (slot_gate > 0.0).astype(F32).astype(BF)

        def order(at):
            nth = ((at >> 3) & 3) * 4 + (at & 3)
            far = (nth + 1) >> 1
            place = (z + jnp.where((nth & 1) == 1, -far, far) + 16) & 15
            return place * 8 + (at >> 5)

        to, source = iota((256, 256), 0), iota((256, 256), 1)
        before = ((order(source) < order(to)) & ((source & 4) == 0)).astype(F32).astype(BF)
        pair = (lane_c >> 1) == (lane_w >> 1)
        first = (pair & (lane_c < lane_w)).astype(F32).astype(BF)
        pair = pair.astype(F32).astype(BF)
        rank = dot(before, dot(taken, pair).astype(BF)) + dot(taken, first)
        limit_0 = cap_ref[2 * row].astype(F32)
        limit_1 = cap_ref[2 * row + 1].astype(F32)
        lanes = iota((256, 128), 1)
        limit = jnp.where(((lanes >> 1) & 1) == 0, limit_0, limit_1)
        kept = jnp.where(rank < limit, slot_gate, 0.0)
        second = (iota((256, 1), 0) & 4) != 0
        for p in range(2):
            slots = [
                jnp.sum(jnp.where(lanes == 4 * me + 2 * p + t, kept, 0.0), axis=1, keepdims=True) for t in range(2)
            ]
            column = jnp.where(second, slots[1], slots[0])
            for b in range(BLOCKS):
                piece = jnp.concatenate([column[32 * d + 8 * b : 32 * d + 8 * b + 8] for d in range(8)], axis=0)
                KW[b, p] = jnp.broadcast_to(piece, (64, 128))

    select(0)
    place_slots(1)
    select(1)
    place_slots(2)
    select(2)
    place_slots(3)
    GS[me] = GM[...]
    moved_g = [remote(GM, GS.at[me], at_y(k)) for k in range(1, 8)]
    select(3)
    for copy in own_w:
        copy.wait()
    for copy in moved_w:
        copy.wait_recv()
    products(0)
    products(1)
    products(2)
    weigh()
    activate(0)
    products(3)
    activate(1)
    down(0)
    activate(2)
    down(1)
    activate(3)
    down(2)
    combine(0)
    leaves(0)
    down(3)
    combine(1)
    leaves(1)
    combine(2)
    leaves(2)
    combine(3)
    leaves(3)

    for via in (-1, 1, 3, -3, 5, -6):
        total = C[PLACE[via]]
        for delta, v in RELAY.items():
            if v == via:
                back_z[delta].wait_recv()
                total = total + T[PLACE[delta]].astype(F32)
        CB[PLACE[via]] = total.astype(BF)
        give(via, 0)
    mixed = SM[...] + C[0]
    for via in (-1, 1, 3, -3, 5, -6):
        back_z[via].wait_recv()
        mixed = mixed + T[PLACE[via]].astype(F32)

    mixed = jnp.concatenate([mixed[0:ROWS], mixed[ROWS:CH]], axis=1)
    for k in range(4):
        FX[k] = jnp.concatenate([mixed[6 * k : 6 * k + 6], jnp.zeros((2, DX), F32)], axis=0)
    FO[x] = FX[x]
    last = [remote(FX.at[xs[k]], FO.at[x], at_x(k)) for k in (2, 1, 3)]
    for copy in last:
        copy.wait_recv()
    for k in range(4):
        out_ref[:, DX * k : DX * k + DX] = FO[k, 0:6].astype(BF)
    for copy in sent:
        copy.wait_send()


def on_device(
    residual, queries, keys, values, out_gate, decay_input, beta_input, decay_log, decay_bias, past_state,
    head_norm, out_proj, post_norm, expert_ids, expert_gates, capacity, gate_proj, up_proj, down_proj,
):
    vmem = pl.BlockSpec(memory_space=pltpu.VMEM)
    hbm = pl.BlockSpec(memory_space=pl.ANY)
    scratch = [
        pltpu.VMEM((ROWS, DX), BF),
        pltpu.VMEM((ROWS, 256), BF),
        pltpu.VMEM((ROWS, 256), BF),
        pltpu.VMEM((ROWS, DX), BF),
        pltpu.VMEM((ROWS, DX), BF),
        pltpu.VMEM((HEADS, ROWS), F32),
        pltpu.VMEM((HEADS, ROWS), F32),
        pltpu.VMEM((1, HEADS), F32),
        pltpu.VMEM((1, HEADS), F32),
        pltpu.VMEM((1, 128), F32),
        pltpu.VMEM((1, DX), F32),
        pltpu.VMEM((TOPK, ROWS), jnp.int32),
        pltpu.VMEM((TOPK, ROWS), F32),
        pltpu.SMEM((256,), jnp.int32),
        pltpu.VMEM((128, 128), F32),
        pltpu.VMEM((ROWS, HEADS, 128, 128), BF),
        pltpu.VMEM((4, DX, DX), BF),
        pltpu.VMEM((4, DX, 256), BF),
        pltpu.VMEM((4, 128, DX), BF),
        pltpu.VMEM((16, 8, 128), F32),
        pltpu.VMEM((2, 8 * ROWS, 128), F32),
        pltpu.VMEM((HEADS, 8 * ROWS, 128), F32),
        pltpu.VMEM((4, ROWS, DX), F32),
        pltpu.VMEM((3, ROWS, DX), F32),
        pltpu.VMEM((CH, CW), F32),
        pltpu.VMEM((16, CH, CW), BF),
        pltpu.VMEM((BLOCKS, 4, CH, 128), BF),
        pltpu.VMEM((BLOCKS, 4, CH, 128), BF),
        pltpu.VMEM((BLOCKS, 128, 4 * CH), BF),
        pltpu.VMEM((BLOCKS, 128, 4 * CH), BF),
        pltpu.VMEM((BLOCKS, 8, 16, DX), BF),
        pltpu.VMEM((BLOCKS, 8, 16, DX), BF),
        pltpu.VMEM((16 * ROWS, 128), F32),
        pltpu.VMEM((16 * ROWS, 128), F32),
        pltpu.VMEM((32, 128), F32),
        pltpu.VMEM((8, 32, 128), F32),
        pltpu.VMEM((BLOCKS, 2, 64, 128), F32),
        pltpu.VMEM((BLOCKS, 4, 64, 256), BF),
        pltpu.VMEM((BLOCKS, 3, 64, 256), BF),
        pltpu.VMEM((BLOCKS, 8, 128), F32),
        pltpu.VMEM((BLOCKS, 3, 8, 128), F32),
        pltpu.VMEM((BLOCKS, 4, 64, 128), BF),
        pltpu.VMEM((BLOCKS, 8, 16, DX), BF),
        pltpu.VMEM((BLOCKS, 8, 16, DX), BF),
        pltpu.VMEM((16, CH, CW), F32),
        pltpu.VMEM((16, CH, CW), BF),
        pltpu.VMEM((16, CH, CW), BF),
        pltpu.VMEM((4, 8, DX), F32),
        pltpu.VMEM((4, 8, DX), F32),
        pltpu.SemaphoreType.DMA((N_SEM,)),
        pltpu.SemaphoreType.DMA((N_SEM,)),
        pltpu.SemaphoreType.DMA((32,)),
    ]
    return pl.pallas_call(
        kernel,
        out_shape=pltpu.VMEM((6, 2048), BF),
        in_specs=[hbm] * 19,
        out_specs=vmem,
        scratch_shapes=scratch,
        compiler_params=pltpu.CompilerParams(
            collective_id=1, has_side_effects=True, vmem_limit_bytes=60 * 1024 * 1024
        ),
        name="layer",
    )(
        *[pltpu.with_memory_space_constraint(array, pltpu.HBM) for array in (
        residual, queries, keys, values, out_gate, decay_input.T, beta_input.T, decay_log[None, :], decay_bias[None, :],
        head_norm[None, :], post_norm[None, :], expert_ids.T, expert_gates.T, capacity,
        past_state, out_proj, gate_proj, up_proj, down_proj,
        )]
    )


def solution(mesh):
    placed = (
        P("row", None),
        P("row", "head"),
        P("row", "head"),
        P("row", "head"),
        P("row", "head"),
        P("row", "head"),
        P("row", "head"),
        P("head"),
        P("head"),
        P("row", "head", None, None),
        P(),
        P("head", None),
        P(),
        P("row", None),
        P("row", None),
        P(),
        P("row", None, "head"),
        P("row", None, "head"),
        P("row", "head", None),
    )
    return jax.shard_map(
        on_device, mesh=mesh, in_specs=placed, out_specs=P(("row", "head"), None), check_vma=False
    )
```

```python
import jax
import jax.numpy as jnp
from jax import lax
from jax.experimental import pallas as pl
from jax.experimental.pallas import tpu as pltpu
from jax.sharding import PartitionSpec as P

MESH = pl.DeviceIdType.MESH
BF = jnp.bfloat16
F32 = jnp.float32
HIGH = lax.Precision.HIGHEST

ROWS = 24
TOPK = 10
HEADS = 4
DX = 512
CH, CW = 48, 256
STEP = 4

ORDER = (0, -1, 1, -2, 2, -3, 3, -4, 4, -5, 5, -6, 6, -7, 7, -8)
PLACE = {delta: place for place, delta in enumerate(ORDER)}
DIRECT = (-6, 5, -3, 3, -1, 1)
RELAY = {-2: -1, 2: 1, -4: -3, -5: -3, 4: 3, 6: 5, 7: 5, -7: -6, -8: -6}
REACH = (-6, -5, -3, -2, -1, 1, 2, 3, 5, 6)
BLOCKS = 4
LEAVES = ((-2,), (-4, 2), (-5, 4), (-8, -7, 7, 6))
N_SEM = 192
GATE_AT, DECAY_AT, BETA_AT = 16, 32, 40


def dot(a, b):
    return jnp.dot(a, b, preferred_element_type=F32)


def iota(shape, dim):
    return lax.broadcasted_iota(jnp.int32, shape, dim)


def sigmoid(v):
    return 1.0 / (1.0 + jnp.exp(-v))


def kernel(
    res_hbm, q_hbm, k_hbm, v_hbm, og_hbm, di_hbm, bi_hbm, dl_hbm, db_hbm, hn_hbm, pn_hbm,
    ids_hbm, eg_hbm, cap_hbm, state_hbm, op_hbm, gp_hbm, up_hbm, dp_hbm,
    out_ref,
    res_ref, q_ref, k_ref, v_ref, og_ref, di_ref, bi_ref, dl_ref, db_ref, hn_ref, pn_ref, ids_ref, eg_ref, cap_ref,
    NT,
    ST, OP, W, D, MG, AQ, RD, AP, AR, SM, G, PTL, PTR, PL, PR, S, R, MT, GT, GM, GS, KW,
    MS, MR, SSB, SSR, IN, Y, R2, C, CB, T, FX, FO,
    ss, rs, ls,
):
    row = lax.axis_index("row")
    x = lax.axis_index("head")
    z = row // 8
    me = row % 8
    xs = [x] + [(x + k) % 4 for k in range(1, 4)]
    ds = [me] + [(me + k) % 8 for k in range(1, 8)]

    def at_z(off):
        return (((z + 16 + off) % 16) * 8 + me, x)

    def at_y(k):
        return (z * 8 + ds[k], x)

    def at_x(k):
        return (row, xs[k])

    sent = []

    def remote(src, dst, device):
        n = len(sent)
        copy = pltpu.make_async_remote_copy(
            src_ref=src, dst_ref=dst, send_sem=ss.at[n], recv_sem=rs.at[n], device_id=device, device_id_type=MESH
        )
        copy.start()
        sent.append(copy)
        return copy

    n_local = [0]

    def local(src, dst):
        copy = pltpu.make_async_copy(src, dst, ls.at[n_local[0]])
        n_local[0] += 1
        copy.start()
        return copy

    def x_cols(k):
        return pl.ds(pl.multiple_of(xs[k] * DX, DX), DX)

    barrier = pltpu.get_barrier_semaphore()
    peers = [at_z(off) for off in REACH] + [at_y(k) for k in range(1, 8)] + [at_x(k) for k in range(1, 4)]
    for device in peers:
        pl.semaphore_signal(barrier, inc=1, device_id=device, device_id_type=MESH)

    lists = [local(ids_hbm, ids_ref), local(eg_hbm, eg_ref), local(di_hbm, di_ref), local(bi_hbm, bi_ref)]
    heads = [
        local(a, b)
        for a, b in (
            (q_hbm, q_ref), (k_hbm, k_ref), (v_hbm, v_ref), (og_hbm, og_ref), (dl_hbm, dl_ref), (db_hbm, db_ref),
            (hn_hbm, hn_ref),
        )
    ]
    states = [local(state_hbm.at[pl.ds(STEP * i, STEP)], ST.at[pl.ds(STEP * i, STEP)]) for i in range(ROWS // STEP)]
    later = [local(cap_hbm, cap_ref), local(res_hbm.at[:, x_cols(0)], res_ref), local(pn_hbm.at[:, x_cols(0)], pn_ref)]
    projs = [local(op_hbm.at[:, x_cols(k)], OP.at[k]) for k in (2, 1, 3, 0)]
    own_w = [
        local(gp_hbm.at[0, x_cols(0), :], W.at[x, :, pl.ds(0, 128)]),
        local(up_hbm.at[0, x_cols(0), :], W.at[x, :, pl.ds(128, 128)]),
        local(dp_hbm.at[0, :, x_cols(0)], D.at[x]),
    ]

    for copy in lists:
        copy.wait()
    NT[...] = jnp.zeros((128, 128), F32)
    NT[0:TOPK, 0:ROWS] = ids_ref[...].astype(F32)
    NT[GATE_AT : GATE_AT + TOPK, 0:ROWS] = eg_ref[...]
    NT[DECAY_AT : DECAY_AT + HEADS, 0:ROWS] = di_ref[...]
    NT[BETA_AT : BETA_AT + HEADS, 0:ROWS] = bi_ref[...]
    narrow = jnp.transpose(NT[...])[0:ROWS]
    MG[0] = jnp.concatenate([narrow[8 * g : 8 * g + 8, 0:32] for g in range(3)] + [jnp.zeros((8, 32), F32)], axis=1)

    def direct(buf):
        return {a: remote(buf.at[0], buf.at[PLACE[a]], at_z(-a)) for a in DIRECT}

    def relay(buf, copies, via):
        copies[via].wait_recv()
        for delta, v in RELAY.items():
            if v == via:
                copies[delta] = remote(buf.at[PLACE[v]], buf.at[PLACE[delta]], at_z(v - delta))


    for copy in heads:
        copy.wait()
    q_unit, k_unit, cross = [], [], []
    for g in range(2):
        for ref, scale, units, base in ((q_ref, 128 ** (-0.5), q_unit, 0), (k_ref, 1.0, k_unit, 2)):
            block = ref[:, 128 * g : 128 * g + 128].astype(F32)
            unit = block * (lax.rsqrt(jnp.sum(block * block, axis=1, keepdims=True) + 1e-06) * scale)
            high = unit.astype(BF).astype(F32)
            AQ[g, pl.ds(base, ROWS, stride=8), :] = high
            AQ[g, pl.ds(base + 1, ROWS, stride=8), :] = unit - high
            units.append(unit)
        for spare in range(4, 8):
            AQ[g, pl.ds(spare, ROWS, stride=8), :] = jnp.zeros((ROWS, 128), F32)
        cross.append(jnp.sum(q_unit[g] * k_unit[g], axis=1, keepdims=True))

    def read_rows(i):
        for u in range(STEP):
            r = STEP * i + u
            at = pl.ds(pl.multiple_of(r * 8, 8), 8)
            for g in range(2):
                a = AQ[g, at, :].astype(BF)
                for h in (2 * g, 2 * g + 1):
                    RD[h, at, :] = dot(a, ST[r, h])

    for copy in states:
        copy.wait()
    pl.loop(0, ROWS // STEP)(read_rows)
    pl.semaphore_wait(barrier, len(peers))
    meta = direct(MG)
    moved_w = [remote(gp_hbm.at[0, x_cols(k), :], W.at[x, :, pl.ds(0, 128)], at_x(k)) for k in (1, 3)]

    gated = []
    for h in range(HEADS):
        g = h // 2
        read_q = RD[h, pl.ds(0, ROWS, stride=8), :] + RD[h, pl.ds(1, ROWS, stride=8), :]
        read_k = RD[h, pl.ds(2, ROWS, stride=8), :] + RD[h, pl.ds(3, ROWS, stride=8), :]
        arg = narrow[:, DECAY_AT + h : DECAY_AT + h + 1] + db_ref[:, h : h + 1]
        soft = jnp.maximum(arg, 0.0) + jnp.log(1.0 + jnp.exp(-jnp.abs(arg)))
        decay = jnp.exp(-jnp.exp(dl_ref[:, h : h + 1]) * soft)
        beta = sigmoid(narrow[:, BETA_AT + h : BETA_AT + h + 1])
        cols = slice(128 * h, 128 * h + 128)
        update = beta * (v_ref[:, cols].astype(F32) - decay * read_k)
        head_out = decay * read_q + cross[g] * update
        norm = head_out * lax.rsqrt(jnp.mean(head_out * head_out, axis=1, keepdims=True) + 1e-06) * hn_ref[...]
        gate = og_ref[:, cols].astype(F32)
        gated.append((norm * (gate * sigmoid(gate))).astype(BF))
    gated = jnp.concatenate(gated, axis=1)

    moved_a = {}
    for copy, k in zip(projs, (2, 1, 3, 0)):
        copy.wait()
        AP[k] = dot(gated, OP[k])
        if k:
            moved_a[k] = remote(AP.at[k], AR.at[k - 1], at_x(k))

    for via in (-1, 1, -3, 3):
        relay(MG, meta, via)

    for k in (1, 3, 2):
        moved_a[k].wait_recv()
    for copy in later:
        copy.wait()
    gain = pn_ref[...]
    inverse = 1.0 / gain
    stream = res_ref[...].astype(F32) + ((AP[0] + AR[0]) + (AR[1] + AR[2]))
    SM[...] = jnp.concatenate([stream[:, :CW], stream[:, CW:]], axis=0)
    scaled = stream * gain
    G[0] = jnp.concatenate([scaled[:, :CW], scaled[:, CW:]], axis=0).astype(BF)
    rows_z = direct(G)
    moved_w.append(remote(gp_hbm.at[0, x_cols(2), :], W.at[x, :, pl.ds(0, 128)], at_x(2)))
    for k in (2, 1, 3):
        moved_w.append(remote(up_hbm.at[0, x_cols(k), :], W.at[x, :, pl.ds(128, 128)], at_x(k)))
    moved_d = [remote(dp_hbm.at[0, :, x_cols(k)], D.at[x], at_x(k)) for k in (2, 1, 3)]

    for via in (5, -6):
        relay(MG, meta, via)
    for via in (-1, 1, -3, 3):
        relay(G, rows_z, via)
    for delta in RELAY:
        meta[delta].wait_recv()
    lane = iota((ROWS, 128), 1)
    lane_expert = jnp.where(lane < 32, 16 * z + (lane >> 1), -1).astype(F32)[0:8]

    def name_slots(i):
        for u in range(4):
            j = 4 * i + u
            info = MG[j]
            for g in range(3):
                match = jnp.zeros((8, 128), F32)
                gates = jnp.zeros((8, 128), F32)
                for k in range(TOPK):
                    same = info[:, 32 * g + k : 32 * g + k + 1] == lane_expert
                    match = jnp.where(same, 1.0, match)
                    gates = jnp.where(same, info[:, 32 * g + GATE_AT + k : 32 * g + GATE_AT + k + 1], gates)
                at = pl.ds(pl.multiple_of(j * ROWS + 8 * g, 8), 8)
                MT[at, :] = match
                GT[at, :] = gates

    pl.loop(0, 4)(name_slots)
    later_row = (iota((ROWS, ROWS), 0) > iota((ROWS, ROWS), 1)).astype(F32).astype(BF)
    lane_c, lane_w = iota((128, 128), 0), iota((128, 128), 1)
    spread = ((lane_c >> 1) == (lane_w >> 3)) & ((lane_c & 1) == ((lane_w >> 2) & 1))
    spread = spread.astype(F32).astype(BF)
    lane_slot = (lane & 1).astype(F32)
    lane_place = lane & 3

    def place_slots(b):
        totals = []
        for u in range(4):
            at = slice(ROWS * (4 * b + u), ROWS * (4 * b + u) + ROWS)
            match = MT[at, :]
            here = jnp.where(dot(later_row, match.astype(BF)) == lane_slot, match, 0.0)
            totals.append(jnp.sum(here * GT[at, :], axis=0, keepdims=True))
            placed = jnp.where(lane_place == u, dot(here.astype(BF), spread), 0.0)
            none = jnp.zeros((ROWS, 128), F32)
            PTL[b, u] = jnp.concatenate([placed, none], axis=0).astype(BF)
            PTR[b, u] = jnp.concatenate([none, placed], axis=0).astype(BF)
        GM[8 * b : 8 * b + 8, :] = jnp.concatenate(totals * 2, axis=0)
        PL[b] = jnp.transpose(PTL[b].reshape(4 * CH, 128).astype(F32)).astype(BF)
        PR[b] = jnp.transpose(PTR[b].reshape(4 * CH, 128).astype(F32)).astype(BF)

    place_slots(0)
    for via in (5, -6):
        relay(G, rows_z, via)
    moved_y = []

    def select(b):
        for delta in ORDER[4 * b : 4 * b + 4]:
            if delta and delta not in RELAY.values():
                rows_z[delta].wait_recv()
        chunks = G[4 * b : 4 * b + 4].reshape(4 * CH, CW)
        S[b, :, :, 0:CW] = dot(PL[b], chunks).astype(BF).reshape(8, 16, CW)
        S[b, :, :, CW:DX] = dot(PR[b], chunks).astype(BF).reshape(8, 16, CW)
        moved_y.append([remote(S.at[b, ds[k]], R.at[b, me], at_y(k)) for k in (4, 5, 3, 2, 6, 7, 1)])
        R[b, me] = S[b, me]

    moved_m = []

    def products(b):
        for copy in moved_y[b]:
            copy.wait_recv()
        block = R[b].reshape(128, DX)
        for t in range(4):
            both = dot(block, W[t]).reshape(8, 2, 8, 256)[:, t // 2]
            MS[b, t] = both.reshape(64, 256).astype(BF)
        plain = block.astype(F32) * inverse
        squares = jnp.sum(plain * plain, axis=1, keepdims=True)
        SSB[b] = jnp.transpose(jnp.broadcast_to(squares, (128, 128)))[0:8]
        moved = []
        for k in (2, 1, 3):
            moved.append(remote(MS.at[b, xs[k]], MR.at[b, k - 1], at_x(k)))
            moved.append(remote(SSB.at[b], SSR.at[b, k - 1], at_x(k)))
        moved_m.append(moved)

    moved_i = []

    def activate(b):
        for copy in moved_m[b]:
            copy.wait_recv()
        both = (MS[b, x].astype(F32) + MR[b, 0].astype(F32)) + (MR[b, 1].astype(F32) + MR[b, 2].astype(F32))
        squares = (SSB[b] + SSR[b, 0]) + (SSR[b, 1] + SSR[b, 2])
        squares = jnp.transpose(jnp.concatenate([squares] * 16, axis=0))[:, 0:1].reshape(8, 2, 8, 1)
        squares = jnp.where(x // 2 == 0, squares[:, 0], squares[:, 1]).reshape(64, 1)
        scale = lax.rsqrt(squares * (1.0 / 2048.0) + 1e-06)
        gate = both[:, 0:128] * scale
        up = both[:, 128:256] * scale
        IN[b, x] = (gate * sigmoid(gate) * up).astype(BF)
        moved_i.append([remote(IN.at[b, x], IN.at[b, x], at_x(k)) for k in (2, 1, 3)])

    moved_r = []

    def down(b):
        if b == 0:
            for copy in moved_d:
                copy.wait_recv()
        for copy in moved_i[b]:
            copy.wait_recv()
        parts = []
        for p in range(2):
            inner = jnp.concatenate([IN[b, 2 * p], IN[b, 2 * p + 1]], axis=1)
            part = dot(inner, D[2 * p : 2 * p + 2].reshape(256, DX))
            part = part * jnp.concatenate([KW[b, p]] * 4, axis=1)
            parts.append(part.reshape(8, 8, DX))
        Y[b] = jnp.concatenate(parts, axis=1).astype(BF)
        moved_r.append([remote(Y.at[b, ds[k]], R2.at[b, me], at_y(k)) for k in (4, 5, 3, 2, 6, 7, 1)])
        R2[b, me] = Y[b, me]

    def combine(b):
        for copy in moved_r[b]:
            copy.wait_recv()
        back = R2[b].reshape(128, DX)
        left = dot(PTL[b].reshape(4 * CH, 128), back[:, 0:CW])
        right = dot(PTR[b].reshape(4 * CH, 128), back[:, CW:DX])
        C[4 * b : 4 * b + 4] = (left + right).reshape(4, CH, CW)

    back_z = {}

    def give(delta, via):
        place = PLACE[delta]
        back_z[delta] = remote(CB.at[place], T.at[place], at_z(delta - via))

    def leaves(b):
        for delta in LEAVES[b]:
            CB[PLACE[delta]] = C[PLACE[delta]].astype(BF)
            give(delta, RELAY[delta])

    def weigh():
        for copy in moved_g:
            copy.wait_recv()
        slot_gate = GS[...].reshape(256, 128)
        taken = (slot_gate > 0.0).astype(F32).astype(BF)

        def order(at):
            nth = ((at >> 3) & 3) * 4 + (at & 3)
            far = (nth + 1) >> 1
            place = (z + jnp.where((nth & 1) == 1, -far, far) + 16) & 15
            return place * 8 + (at >> 5)

        to, source = iota((256, 256), 0), iota((256, 256), 1)
        before = ((order(source) < order(to)) & ((source & 4) == 0)).astype(F32).astype(BF)
        pair = (lane_c >> 1) == (lane_w >> 1)
        first = (pair & (lane_c < lane_w)).astype(F32).astype(BF)
        pair = pair.astype(F32).astype(BF)
        rank = dot(before, dot(taken, pair).astype(BF)) + dot(taken, first)
        limit_0 = cap_ref[2 * row].astype(F32)
        limit_1 = cap_ref[2 * row + 1].astype(F32)
        lanes = iota((256, 128), 1)
        limit = jnp.where(((lanes >> 1) & 1) == 0, limit_0, limit_1)
        kept = jnp.where(rank < limit, slot_gate, 0.0)
        second = (iota((256, 1), 0) & 4) != 0
        for p in range(2):
            slots = [
                jnp.sum(jnp.where(lanes == 4 * me + 2 * p + t, kept, 0.0), axis=1, keepdims=True) for t in range(2)
            ]
            column = jnp.where(second, slots[1], slots[0])
            for b in range(BLOCKS):
                piece = jnp.concatenate([column[32 * d + 8 * b : 32 * d + 8 * b + 8] for d in range(8)], axis=0)
                KW[b, p] = jnp.broadcast_to(piece, (64, 128))

    select(0)
    place_slots(1)
    select(1)
    place_slots(2)
    select(2)
    place_slots(3)
    GS[me] = GM[...]
    moved_g = [remote(GM, GS.at[me], at_y(k)) for k in range(1, 8)]
    select(3)
    for copy in own_w:
        copy.wait()
    for copy in moved_w:
        copy.wait_recv()
    products(0)
    products(1)
    products(2)
    products(3)
    weigh()
    activate(0)
    activate(1)
    activate(2)
    activate(3)
    down(0)
    down(1)
    down(2)
    down(3)
    combine(0)
    leaves(0)
    combine(1)
    leaves(1)
    combine(2)
    leaves(2)
    combine(3)
    leaves(3)

    for via in (-1, 1, 3, -3, 5, -6):
        total = C[PLACE[via]]
        for delta, v in RELAY.items():
            if v == via:
                back_z[delta].wait_recv()
                total = total + T[PLACE[delta]].astype(F32)
        CB[PLACE[via]] = total.astype(BF)
        give(via, 0)
    mixed = SM[...] + C[0]
    for via in (-1, 1, 3, -3, 5, -6):
        back_z[via].wait_recv()
        mixed = mixed + T[PLACE[via]].astype(F32)

    mixed = jnp.concatenate([mixed[0:ROWS], mixed[ROWS:CH]], axis=1)
    for k in range(4):
        FX[k] = jnp.concatenate([mixed[6 * k : 6 * k + 6], jnp.zeros((2, DX), F32)], axis=0)
    FO[x] = FX[x]
    last = [remote(FX.at[xs[k]], FO.at[x], at_x(k)) for k in (2, 1, 3)]
    for copy in last:
        copy.wait_recv()
    for k in range(4):
        out_ref[:, DX * k : DX * k + DX] = FO[k, 0:6].astype(BF)
    for copy in sent:
        copy.wait_send()


def on_device(
    residual, queries, keys, values, out_gate, decay_input, beta_input, decay_log, decay_bias, past_state,
    head_norm, out_proj, post_norm, expert_ids, expert_gates, capacity, gate_proj, up_proj, down_proj,
):
    vmem = pl.BlockSpec(memory_space=pltpu.VMEM)
    hbm = pl.BlockSpec(memory_space=pl.ANY)
    scratch = [
        pltpu.VMEM((ROWS, DX), BF),
        pltpu.VMEM((ROWS, 256), BF),
        pltpu.VMEM((ROWS, 256), BF),
        pltpu.VMEM((ROWS, DX), BF),
        pltpu.VMEM((ROWS, DX), BF),
        pltpu.VMEM((HEADS, ROWS), F32),
        pltpu.VMEM((HEADS, ROWS), F32),
        pltpu.VMEM((1, HEADS), F32),
        pltpu.VMEM((1, HEADS), F32),
        pltpu.VMEM((1, 128), F32),
        pltpu.VMEM((1, DX), F32),
        pltpu.VMEM((TOPK, ROWS), jnp.int32),
        pltpu.VMEM((TOPK, ROWS), F32),
        pltpu.SMEM((256,), jnp.int32),
        pltpu.VMEM((128, 128), F32),
        pltpu.VMEM((ROWS, HEADS, 128, 128), BF),
        pltpu.VMEM((4, DX, DX), BF),
        pltpu.VMEM((4, DX, 256), BF),
        pltpu.VMEM((4, 128, DX), BF),
        pltpu.VMEM((16, 8, 128), F32),
        pltpu.VMEM((2, 8 * ROWS, 128), F32),
        pltpu.VMEM((HEADS, 8 * ROWS, 128), F32),
        pltpu.VMEM((4, ROWS, DX), F32),
        pltpu.VMEM((3, ROWS, DX), F32),
        pltpu.VMEM((CH, CW), F32),
        pltpu.VMEM((16, CH, CW), BF),
        pltpu.VMEM((BLOCKS, 4, CH, 128), BF),
        pltpu.VMEM((BLOCKS, 4, CH, 128), BF),
        pltpu.VMEM((BLOCKS, 128, 4 * CH), BF),
        pltpu.VMEM((BLOCKS, 128, 4 * CH), BF),
        pltpu.VMEM((BLOCKS, 8, 16, DX), BF),
        pltpu.VMEM((BLOCKS, 8, 16, DX), BF),
        pltpu.VMEM((16 * ROWS, 128), F32),
        pltpu.VMEM((16 * ROWS, 128), F32),
        pltpu.VMEM((32, 128), F32),
        pltpu.VMEM((8, 32, 128), F32),
        pltpu.VMEM((BLOCKS, 2, 64, 128), F32),
        pltpu.VMEM((BLOCKS, 4, 64, 256), BF),
        pltpu.VMEM((BLOCKS, 3, 64, 256), BF),
        pltpu.VMEM((BLOCKS, 8, 128), F32),
        pltpu.VMEM((BLOCKS, 3, 8, 128), F32),
        pltpu.VMEM((BLOCKS, 4, 64, 128), BF),
        pltpu.VMEM((BLOCKS, 8, 16, DX), BF),
        pltpu.VMEM((BLOCKS, 8, 16, DX), BF),
        pltpu.VMEM((16, CH, CW), F32),
        pltpu.VMEM((16, CH, CW), BF),
        pltpu.VMEM((16, CH, CW), BF),
        pltpu.VMEM((4, 8, DX), F32),
        pltpu.VMEM((4, 8, DX), F32),
        pltpu.SemaphoreType.DMA((N_SEM,)),
        pltpu.SemaphoreType.DMA((N_SEM,)),
        pltpu.SemaphoreType.DMA((32,)),
    ]
    return pl.pallas_call(
        kernel,
        out_shape=pltpu.VMEM((6, 2048), BF),
        in_specs=[hbm] * 19,
        out_specs=vmem,
        scratch_shapes=scratch,
        compiler_params=pltpu.CompilerParams(
            collective_id=1, has_side_effects=True, vmem_limit_bytes=60 * 1024 * 1024
        ),
        name="layer",
    )(
        *[pltpu.with_memory_space_constraint(array, pltpu.HBM) for array in (
        residual, queries, keys, values, out_gate, decay_input.T, beta_input.T, decay_log[None, :], decay_bias[None, :],
        head_norm[None, :], post_norm[None, :], expert_ids.T, expert_gates.T, capacity,
        past_state, out_proj, gate_proj, up_proj, down_proj,
        )]
    )


def solution(mesh):
    placed = (
        P("row", None),
        P("row", "head"),
        P("row", "head"),
        P("row", "head"),
        P("row", "head"),
        P("row", "head"),
        P("row", "head"),
        P("head"),
        P("head"),
        P("row", "head", None, None),
        P(),
        P("head", None),
        P(),
        P("row", None),
        P("row", None),
        P(),
        P("row", None, "head"),
        P("row", None, "head"),
        P("row", "head", None),
    )
    return jax.shard_map(
        on_device, mesh=mesh, in_specs=placed, out_specs=P(("row", "head"), None), check_vma=False
    )
```
